256 devices in a mesh: lon: 8 (over z), lat: 16 (over y, x), span: 2 (over core).
Axes of the slice: x: 4, y: 4, z: 8, core: 2. Of those that a mesh axis runs over, the one named last changes fastest.
Arguments:
- state: float32 [2, 64, 256, 4096], P(None, None, 'lat', ('lon', 'span')), may hold values from -6 to 6
- winds: float32 [2, 64, 256, 4096], P(None, None, 'lat', ('lon', 'span')), may hold values from -0.45 to 0.45
- memory: bfloat16 [1048576, 128], P(('lon', 'lat', 'span')), may hold values from -6 to 6
- w_in: bfloat16 [256, 512], replicated, may hold values from -0.375 to 0.375
- w_mid: bfloat16 [512, 512], replicated, may hold values from -0.25 to 0.25
- w_deep: bfloat16 [512, 512], replicated, may hold values from -0.25 to 0.25
- w_out: bfloat16 [512, 256], replicated, may hold values from -0.25 to 0.25
- dest: int32 [256, 4096], P('lat', ('lon', 'span')), may hold values from 0 to 31, as said below
- slot: int32 [256, 4096], P('lat', ('lon', 'span')), may hold values from 0 to 127, as said below
- convect: int32 [256, 4096], P('lat', ('lon', 'span')), may hold values from 0 to 1
Outputs:
- new_state: float32 [2, 64, 256, 4096], P(None, None, 'lat', ('lon', 'span'))
- new_memory: bfloat16 [1048576, 128], P(('lon', 'lat', 'span'))
The draws below stay inside these ranges and needn't reach their ends.
Inputs may be any that keep to these rules, and one draw needn't show every extreme that they name: `dest`: owner of a column among the 32 devices of the same lon index, numbered lat index * 2 + span index. The columns of one device with convect 1 and one owner hold slots 0 to n - 1, each once, with n at most 128; in every lon index some owner gets exactly 128 such columns from every device. `slot`: slot of a column at its owner, see dest.
All inputs are finite; a program needn't handle non-finite values.
Results may differ from the reference program's by a relative error of at most 0.003.
Values may be sent and summed in bfloat16 or wider, within the bound.
No kernel may reach another device: no remote copies, remote signals or barrier semaphores. Data moves between devices by JAX's collectives and lax.ppermute only.
A program may use at most 64 MiB of HBM per device.

```python
import jax
import jax.numpy as jnp
from jax import lax

LEV = 64
HID = 512
CY = 16
CX = 256
FEAT = 128
OWNERS = 2
GROUP = 32
COLS_DEV = 4096
CAP = 128
NY = 256
NX = 4096
SLOTS = 1048576


def lay_out(values):
    tiles_lat = NY // CY
    tiles_lon = NX // CX
    return values.reshape(tiles_lat, tiles_lon, CY, CX).transpose(0, 2, 1, 3).reshape(NY, NX)


def balance_lists(key):
    tiles_lat = NY // CY
    tiles_lon = NX // CX
    count_key, busy_key, order_key = jax.random.split(key, 3)
    counts = jax.random.randint(count_key, (tiles_lat, tiles_lon, GROUP), 0, 4 * CAP // 5 + 1)
    busy = jax.random.randint(busy_key, (tiles_lon // OWNERS,), 0, GROUP)
    busy_tile = jnp.repeat(busy, OWNERS)
    owners_all = jnp.arange(GROUP, dtype=jnp.int32)
    counts = jnp.where(owners_all[None, None, :] == busy_tile[None, :, None], CAP, counts)
    scores = jax.random.randint(order_key, (tiles_lat, tiles_lon, COLS_DEV), 0, 2 ** 30 // COLS_DEV)
    scores = scores * COLS_DEV + jnp.arange(COLS_DEV, dtype=jnp.int32)
    places = jnp.argsort(scores, axis=-1).astype(jnp.int32)
    target = places // CAP
    within = places % CAP
    limit = jnp.take_along_axis(counts, target, axis=-1)
    active = (within < limit).astype(jnp.int32)
    return (lay_out(target), lay_out(within), lay_out(active))


def draw_dest(key, part):
    lists = balance_lists(key)
    return lists[0].astype(jnp.int32)


def draw_slot(key, part):
    lists = balance_lists(key)
    return lists[1].astype(jnp.int32)


def draw_convect(key, part):
    lists = balance_lists(key)
    return lists[2].astype(jnp.int32)


def level_of(stream_key, shape, shards, least, high):
    gain, own = 1.0, jax.random.fold_in(stream_key, 6)
    for axis_at, blocks in shards:
        draws = jnp.exp(jax.random.uniform(jax.random.fold_in(own, axis_at), (blocks,), jnp.float32, least / len(shards), high / len(shards)))
        gain = gain * jnp.repeat(draws, shape[axis_at] // blocks).reshape([-1 if axis == axis_at else 1 for axis in range(len(shape))])
    return gain


def noise(own_key, extent, deviation, most, pieces=(), kind=jnp.bfloat16):
    array = jax.random.normal(own_key, extent, jnp.float32) * deviation
    if len(pieces) > 0:
        array = level_of(own_key, extent, pieces, -0.22, 0.18) * array
    return jnp.clip(array, min=-most, max=most).astype(kind)


def setup_inputs(seed: int = 0) -> dict:
    arg_keys = jax.random.split(jax.random.key(seed), 11)
    state = noise(arg_keys[0], (2, LEV, NY, NX), 1.0, 6.0, ((2, 16), (3, 16)), jnp.float32)
    winds = jnp.clip(jax.random.uniform(arg_keys[1], (2, LEV, NY, NX), jnp.float32, -0.45, 0.45) * level_of(arg_keys[1], (2, LEV, NY, NX), ((2, 16), (3, 16)), -0.4, 0.0), -0.45, 0.45)
    memory = noise(arg_keys[2], (SLOTS, FEAT), 1.0, 6.0, ((0, 256),))
    w_in = noise(arg_keys[3], (2 * FEAT, HID), (2 * FEAT) ** -0.5, 0.375)
    w_mid = noise(arg_keys[4], (HID, HID), HID ** -0.5, 0.25)
    w_deep = noise(arg_keys[5], (HID, HID), HID ** -0.5, 0.25)
    w_out = noise(arg_keys[6], (HID, 2 * FEAT), HID ** -0.5, 0.25)
    dest = draw_dest(jax.random.fold_in(arg_keys[10], 71), 0)
    slot = draw_slot(jax.random.fold_in(arg_keys[10], 71), 0)
    convect = draw_convect(jax.random.fold_in(arg_keys[10], 71), 0)
    return {"state": state, "winds": winds, "memory": memory, "w_in": w_in, "w_mid": w_mid, "w_deep": w_deep, "w_out": w_out, "dest": dest, "slot": slot, "convect": convect}


def advect(state, winds):
    west = jnp.roll(state, 1, axis=3)
    east = jnp.roll(state, -1, axis=3)
    padded = jnp.pad(state, ((0, 0), (0, 0), (1, 1), (0, 0)))
    south = padded[:, :, :-2, :]
    north = padded[:, :, 2:, :]
    zonal = winds[0][None]
    meridional = winds[1][None]
    return (state - jnp.maximum(zonal, 0.0) * (state - west) - jnp.minimum(zonal, 0.0) * (east - state)
            - jnp.maximum(meridional, 0.0) * (state - south) - jnp.minimum(meridional, 0.0) * (north - state))


def column_mlp(columns, recalled, w_in, w_mid, w_deep, w_out):
    joined = jnp.concatenate([columns, recalled], axis=1)
    first = jax.nn.silu(jnp.dot(joined, w_in, preferred_element_type=jnp.float32)).astype(jnp.bfloat16)
    second = jax.nn.silu(jnp.dot(first, w_mid, preferred_element_type=jnp.float32)).astype(jnp.bfloat16)
    third = jax.nn.silu(jnp.dot(second, w_deep, preferred_element_type=jnp.float32)).astype(jnp.bfloat16)
    result = jnp.dot(third, w_out, preferred_element_type=jnp.float32)
    width = columns.shape[1]
    tendency = result[:, :width].astype(jnp.bfloat16)
    renewed = (recalled.astype(jnp.float32) + result[:, width:]).astype(jnp.bfloat16)
    return tendency, renewed


def reference(state, winds, memory, w_in, w_mid, w_deep, w_out, dest, slot, convect):
    dynamics = advect(state, winds)
    total = NY * NX
    columns = state.reshape(FEAT, total).T.astype(jnp.bfloat16)
    lat_cell = jnp.arange(NY, dtype=jnp.int32)[:, None]
    lon_block = jnp.arange(NX, dtype=jnp.int32)[None, :] // CX
    source = (lat_cell // CY) * OWNERS + lon_block % OWNERS
    home = ((lon_block // OWNERS) * GROUP + dest) * COLS_DEV + source * CAP + slot
    home = home.reshape(total).astype(jnp.int32)
    recalled = memory[home]
    blocks = total // COLS_DEV

    def run_block(pair):
        return column_mlp(pair[0], pair[1], w_in, w_mid, w_deep, w_out)

    tendency, renewed = lax.map(run_block, (columns.reshape(blocks, COLS_DEV, FEAT), recalled.reshape(blocks, COLS_DEV, FEAT)))
    tendency = tendency.reshape(total, FEAT)
    renewed = renewed.reshape(total, FEAT)
    live = convect.reshape(total) > 0
    parked = jnp.where(live, home, SLOTS).astype(jnp.int32)
    new_memory = memory.at[parked].set(renewed, mode="drop")
    change = jnp.where(live[:, None], tendency.astype(jnp.float32), 0.0)
    new_state = dynamics + change.T.reshape(2, LEV, NY, NX)
    return new_state, new_memory
```

```python
import jax
import jax.numpy as jnp
from jax import lax
from jax.experimental import pallas as pl
from jax.experimental.pallas import tpu as pltpu
from jax.sharding import PartitionSpec as P

GROUP_AXES = ("lat", "span")
MIB = 1024 * 1024
ROWS_MLP = 2048
PART = 1024
VMEM_LIMIT = 60 * MIB
SUB = 8


def swapped(edge, axis, first, wrap):
    count = lax.axis_size(axis)
    pairs = [(i, (i + 1) % count) for i in range(first, count if wrap else count - 1, 2)]
    return lax.ppermute(edge, axis, pairs + [(j, i) for i, j in pairs])


def exchange(rows):
    return lax.all_to_all(rows, GROUP_AXES, split_axis=0, concat_axis=0, tiled=True)


def tile_row(y, half):
    return (y // SUB) * (2 * SUB) + half * SUB + y % SUB


def one_hot(index, size):
    place = lax.broadcasted_iota(jnp.int32, (size, index.shape[1]), 0)
    return (place == index).astype(jnp.bfloat16)


def log2(size):
    return size.bit_length() - 1


def dispatch_kernel(
    ny,
    nx,
    dest,
    slot,
    convect,
    state_hbm,
    slots,
    lat_even,
    lat_odd,
    lon_even,
    lon_odd,
    target,
    filled,
    state,
    chosen,
    choice,
    total,
    edges,
    arrived,
):
    load = pltpu.make_async_copy(state_hbm, state, arrived)
    load.start()
    width = state.shape[0] // (ny * 2)
    lanes = nx // 2
    lower = choice.shape[1]
    uppers = chosen.shape[2] // width
    depth = choice.shape[2]
    lines = depth // nx
    steps = ny // lines
    group = filled.shape[0]
    capacity = ny * nx // group
    shift, mask = log2(lower), lower - 1
    live = convect[...] > 0
    goal = jnp.where(live, dest[...] * capacity + slot[...], ny * nx)
    owner = goal >> log2(capacity)
    owners = lax.broadcasted_iota(jnp.int32, (group, nx), 0)
    counts = jnp.zeros((group, nx), jnp.int32)
    for y in range(ny):
        counts += (owners == owner[y : y + 1]).astype(jnp.int32)
    filled[...] = jnp.broadcast_to(jnp.sum(counts, axis=1, keepdims=True), filled.shape)
    for half in range(2):
        target[half] = goal[:, half * lanes : (half + 1) * lanes]
    goals = goal.T
    load.wait()

    def build(g, b):
        for line in range(lines):
            y = g * lines + line
            choice[b, :, pl.ds(line * nx, nx)] = one_hot(goal[y : y + 1] & mask, lower)
            upper = jnp.broadcast_to(goals[:, y : y + 1] >> shift, (nx, width))
            for half in range(2):
                part = slice(half * lanes, (half + 1) * lanes)
                values = state[pl.ds(tile_row(y, half), width, stride=2 * ny), :].T
                if half == 0:
                    edges[pl.ds(y, 1), :] = values[:1]
                else:
                    edges[pl.ds(ny + y, 1), :] = values[lanes - 1 :]
                values = values.astype(jnp.bfloat16)
                rows = pl.ds(line * nx + half * lanes, lanes)
                for h in range(uppers):
                    chosen[b, rows, pl.ds(h * width, width)] = jnp.where(
                        upper[part] == h, values, jnp.zeros_like(values)
                    )

    def multiply(g, b):
        product = jnp.dot(choice[b], chosen[b], preferred_element_type=jnp.float32)
        if g == 0:
            total[...] = product
        else:
            total[...] += product

    build(0, 0)
    for g in range(steps):
        if g < steps - 1:
            build(g + 1, (g + 1) % 2)
        multiply(g, g % 2)
    for h in range(uppers):
        slots[pl.ds(h * lower, lower), :] = total[:, pl.ds(h * width, width)].astype(slots.dtype)

    odd = lax.axis_index("lat") % 2 == 1
    for half in range(2):
        part = pl.ds(half * lanes, lanes)
        south = state[pl.ds(tile_row(0, half), width, stride=2 * ny), :]
        north = state[pl.ds(tile_row(ny - 1, half), width, stride=2 * ny), :]
        lat_even[:, part] = jnp.where(odd, south, north).astype(lat_even.dtype)
        lat_odd[:, part] = jnp.where(odd, north, south).astype(lat_odd.dtype)
    odd = lax.axis_index("span") == 1
    west, east = edges[pl.ds(0, ny), :], edges[pl.ds(ny, ny), :]
    lon_even[...] = jnp.where(odd, west, east).astype(lon_even.dtype)
    lon_odd[...] = jnp.where(odd, east, west).astype(lon_odd.dtype)


def dispatch(dest, slot, convect, state, group):
    ny, nx = dest.shape
    width, count = state.shape[0] // (ny * 2), ny * nx
    uppers, depth = 4, 4 * nx
    lower = count // uppers
    vmem = pl.BlockSpec(memory_space=pltpu.VMEM)
    kernel = lambda *refs: dispatch_kernel(ny, nx, *refs)
    shape = jax.ShapeDtypeStruct
    return pl.pallas_call(
        kernel,
        out_shape=(
            shape((count, width), jnp.bfloat16),
            shape((width, nx), jnp.bfloat16),
            shape((width, nx), jnp.bfloat16),
            shape((ny, width), jnp.bfloat16),
            shape((ny, width), jnp.bfloat16),
            shape((2, ny, nx // 2), jnp.int32),
            shape((group, width), jnp.int32),
        ),
        in_specs=[vmem, vmem, vmem, pl.BlockSpec(memory_space=pl.ANY)],
        out_specs=(vmem,) * 7,
        scratch_shapes=[
            pltpu.VMEM(state.shape, jnp.float32),
            pltpu.VMEM((2, depth, uppers * width), jnp.bfloat16),
            pltpu.VMEM((2, lower, depth), jnp.bfloat16),
            pltpu.VMEM((lower, uppers * width), jnp.float32),
            pltpu.VMEM((2 * ny, width), jnp.float32),
            pltpu.SemaphoreType.DMA,
        ],
        compiler_params=pltpu.CompilerParams(vmem_limit_bytes=63 * MIB),
        cost_estimate=pl.CostEstimate(
            flops=2 * count * count * width,
            bytes_accessed=6 * count * width,
            transcendentals=0,
        ),
        name="dispatch",
    )(dest, slot, convect, state)


def silu(v):
    half = 0.5 * v
    return half + half * jnp.tanh(half)


def network_kernel(capacity, filled, columns, recalled, w_in, w_mid, w_deep, w_out, tend, renewed):
    width = columns.shape[1]
    size, wide = PART, w_out.shape[1]
    parts = columns.shape[0] // size
    rows = [pl.ds(p * size, size) for p in range(parts)]
    values = [[columns[r, :], recalled[r, :]] for r in rows]
    waiting = []

    def settle():
        sums, kept = waiting.pop(0)
        kept.append(silu(sums).astype(jnp.bfloat16))

    for weights in (w_in, w_mid, w_deep):
        following = [[] for _ in rows]
        for p in range(parts):
            joined = jnp.concatenate(values[p], axis=1)
            for n in range(weights.shape[1] // wide):
                piece = weights[:, pl.ds(n * wide, wide)]
                sums = jnp.dot(joined, piece, preferred_element_type=jnp.float32)
                waiting.append((sums, following[p]))
                if len(waiting) > 1:
                    settle()
        values = following
    settle()
    owners = size // capacity
    place = lax.broadcasted_iota(jnp.int32, (capacity, width), 0)
    for p in range(parts):
        joined = jnp.concatenate(values[p], axis=1)
        result = jnp.dot(joined, w_out[...], preferred_element_type=jnp.float32)
        tend[rows[p], :] = result[:, :width].astype(tend.dtype)
        for o in range(owners):
            part = pl.ds(p * size + o * capacity, capacity)
            live = place < filled[pl.ds(p * owners + o, 1), :]
            update = result[o * capacity : (o + 1) * capacity, width:]
            old = recalled[part, :].astype(jnp.float32)
            renewed[part, :] = (old + jnp.where(live, update, 0.0)).astype(renewed.dtype)


def network(filled, columns, recalled, w_in, w_mid, w_deep, w_out):
    count, width = columns.shape
    capacity = count // filled.shape[0]
    rows = pl.BlockSpec((ROWS_MLP, width), lambda i: (i, 0))
    counts = pl.BlockSpec((ROWS_MLP // capacity, width), lambda i: (i, 0))
    whole = lambda w: pl.BlockSpec(w.shape, lambda i: (0, 0))
    kernel = lambda *refs: network_kernel(capacity, *refs)
    weights = (w_in, w_mid, w_deep, w_out)
    return pl.pallas_call(
        kernel,
        grid=(count // ROWS_MLP,),
        out_shape=(
            jax.ShapeDtypeStruct((count, width), jnp.bfloat16),
            jax.ShapeDtypeStruct((count, width), jnp.bfloat16),
        ),
        in_specs=[counts, rows, rows] + [whole(w) for w in weights],
        out_specs=(rows, rows),
        compiler_params=pltpu.CompilerParams(vmem_limit_bytes=VMEM_LIMIT),
        cost_estimate=pl.CostEstimate(
            flops=2 * count * sum(w.size for w in weights),
            bytes_accessed=8 * count * width + 2 * sum(w.size for w in weights),
            transcendentals=count * 3 * w_mid.shape[0],
        ),
        name="network",
    )(filled, columns, recalled, *weights)


def finish_kernel(
    ny,
    nx,
    target,
    tend,
    state_hbm,
    winds_hbm,
    lat_even,
    lat_odd,
    lon_even,
    lon_odd,
    out,
    state,
    winds,
    table,
    low,
    high,
    west,
    east,
    arrived,
):
    width = state.shape[0] // (ny * 2)
    lanes = nx // 2
    subs = ny // SUB
    levels = winds.shape[0] // (4 * ny)
    copies = [
        pltpu.make_async_copy(state_hbm, state, arrived.at[0]),
        pltpu.make_async_copy(winds_hbm, winds, arrived.at[1]),
    ]
    for copy in copies:
        copy.start()
    lower = table.shape[1]
    uppers = table.shape[0] // width
    for h in range(uppers):
        rows = tend[pl.ds(h * lower, lower), :].astype(jnp.float32)
        table[pl.ds(h * width, width), :] = rows.T.astype(table.dtype)
    odd = lax.axis_index("span") == 1
    evens, odds = lon_even[...].astype(jnp.float32), lon_odd[...].astype(jnp.float32)
    west[...] = jnp.where(odd, evens, odds)
    east[...] = jnp.where(odd, odds, evens)
    odd = lax.axis_index("lat") % 2 == 1
    for half in range(2):
        part = pl.ds(half * lanes, lanes)
        evens, odds = lat_even[:, part].astype(jnp.float32), lat_odd[:, part].astype(jnp.float32)
        low[half] = jnp.where(odd, evens, odds)
        high[half] = jnp.where(odd, odds, evens)

    shift, mask = log2(lower), lower - 1

    for y in range(ny):
        index = jnp.concatenate([target[half, pl.ds(y, 1), :] for half in range(2)], axis=1)
        candidates = jnp.dot(
            table[...], one_hot(index & mask, lower), preferred_element_type=jnp.float32
        )
        upper = jnp.broadcast_to(index >> shift, (width, nx))
        change = jnp.zeros((width, nx), jnp.float32)
        for h in range(uppers):
            change = jnp.where(upper == h, candidates[h * width : (h + 1) * width], change)
        for half in range(2):
            place = pl.ds(tile_row(y, half), width, stride=2 * ny)
            out[place, :] = change[:, half * lanes : (half + 1) * lanes]
    for copy in copies:
        copy.wait()

    lane = lax.broadcasted_iota(jnp.int32, (SUB, lanes), 1)
    line = lax.broadcasted_iota(jnp.int32, (SUB, lanes), 0)
    tiles = [(sub, half) for sub in range(subs) for half in range(2)]

    def block(ref, r, sub, half):
        start = pl.multiple_of(r * (2 * ny), 2 * ny) + (sub * 2 + half) * SUB
        return ref.at[pl.ds(start, SUB), :]

    @pl.loop(0, levels, unroll=4)
    def _(k):
        zonal = {t: block(winds, k, *t)[...] for t in tiles}
        meridional = {t: block(winds, levels + k, *t)[...] for t in tiles}
        for f in range(width // levels):
            r = f * levels + k
            s = {t: block(state, r, *t)[...] for t in tiles}
            first = pltpu.roll(west[...], width - r, axis=1)
            last = pltpu.roll(east[...], width - 1 - r, axis=1)
            up = {t: pltpu.roll(s[t], 1, axis=1) for t in tiles}
            down = {t: pltpu.roll(s[t], lanes - 1, axis=1) for t in tiles}
            rise = {t: pltpu.roll(s[t], 1, axis=0) for t in tiles}
            fall = {t: pltpu.roll(s[t], SUB - 1, axis=0) for t in tiles}
            for sub, half in tiles:
                t = (sub, half)
                edge = slice(sub * SUB, (sub + 1) * SUB)
                left = jnp.where(lane == 0, up[sub, 0] if half else first[edge], up[t])
                right = jnp.where(lane == lanes - 1, last[edge] if half else down[sub, 1], down[t])
                under = rise[sub - 1, half] if sub else low[half, pl.ds(r, 1), :]
                over = fall[sub + 1, half] if sub < subs - 1 else high[half, pl.ds(r, 1), :]
                below = jnp.where(line == 0, under, rise[t])
                above = jnp.where(line == SUB - 1, over, fall[t])
                place = block(out, r, *t)
                place[...] = place[...] + (
                    s[t]
                    - jnp.maximum(zonal[t], 0.0) * (s[t] - left)
                    - jnp.minimum(zonal[t], 0.0) * (right - s[t])
                    - jnp.maximum(meridional[t], 0.0) * (s[t] - below)
                    - jnp.minimum(meridional[t], 0.0) * (above - s[t])
                )


def finish(target, tend, state, winds, *edges):
    _, ny, lanes = target.shape
    nx = 2 * lanes
    count, width = tend.shape
    uppers = 8
    vmem = pl.BlockSpec(memory_space=pltpu.VMEM)
    hbm = pl.BlockSpec(memory_space=pl.ANY)
    kernel = lambda *refs: finish_kernel(ny, nx, *refs)
    return pl.pallas_call(
        kernel,
        out_shape=jax.ShapeDtypeStruct(state.shape, jnp.float32),
        in_specs=[vmem, vmem, hbm, hbm, vmem, vmem, vmem, vmem],
        out_specs=vmem,
        scratch_shapes=[
            pltpu.VMEM(state.shape, jnp.float32),
            pltpu.VMEM(winds.shape, jnp.float32),
            pltpu.VMEM((uppers * width, count // uppers), jnp.bfloat16),
            pltpu.VMEM((2, width, nx // 2), jnp.float32),
            pltpu.VMEM((2, width, nx // 2), jnp.float32),
            pltpu.VMEM((ny, width), jnp.float32),
            pltpu.VMEM((ny, width), jnp.float32),
            pltpu.SemaphoreType.DMA((2,)),
        ],
        compiler_params=pltpu.CompilerParams(vmem_limit_bytes=VMEM_LIMIT),
        cost_estimate=pl.CostEstimate(
            flops=2 * count * count * width,
            bytes_accessed=14 * count * width,
            transcendentals=0,
        ),
        name="finish",
    )(target, tend, state, winds, *edges)


def to_tiles(field):
    fields, levels, ny, nx = field.shape
    tiles = field.reshape(fields * levels, ny // SUB, SUB, 2, nx // 2)
    return tiles.transpose(0, 1, 3, 2, 4).reshape(fields * levels * ny * 2, nx // 2)


def from_tiles(tiles, shape):
    fields, levels, ny, nx = shape
    field = tiles.reshape(fields * levels, ny // SUB, 2, SUB, nx // 2)
    return field.transpose(0, 1, 3, 2, 4).reshape(shape)


def body(state, winds, memory, w_in, w_mid, w_deep, w_out, dest, slot, convect):
    group = lax.axis_size(GROUP_AXES)

    recalled = exchange(memory)
    flat_state, flat_winds = to_tiles(state), to_tiles(winds)
    columns, lat_even, lat_odd, lon_even, lon_odd, target, filled = dispatch(
        dest, slot, convect, flat_state, group
    )
    loop = ("lon", "span")
    lon_even = swapped(lon_even, loop, 0, True)
    lon_odd = swapped(lon_odd, loop, 1, True)
    lat_even = swapped(lat_even, "lat", 0, False)
    lat_odd = swapped(lat_odd, "lat", 1, False)
    edges = (lat_even, lat_odd, lon_even)
    columns, edges = lax.optimization_barrier((columns, edges))
    tend, renewed = network(filled, columns, recalled, w_in, w_mid, w_deep, w_out)
    new_memory = exchange(renewed)
    new_state = finish(target, tend, flat_state, flat_winds, *edges, lon_odd)
    return from_tiles(new_state, state.shape), new_memory


def solution(mesh):
    field = P(None, None, "lat", ("lon", "span"))
    slots = P(("lon", "lat", "span"), None)
    plane = P("lat", ("lon", "span"))
    in_specs = (field, field, slots, P(), P(), P(), P(), plane, plane, plane)
    return jax.shard_map(
        body, mesh=mesh, in_specs=in_specs, out_specs=(field, slots), check_vma=False
    )
```

```python
import jax
import jax.numpy as jnp
from jax import lax
from jax.experimental import pallas as pl
from jax.experimental.pallas import tpu as pltpu
from jax.sharding import PartitionSpec as P

GROUP_AXES = ("lat", "span")
MIB = 1024 * 1024
ROWS_MLP = 2048
PART = 1024
VMEM_LIMIT = 60 * MIB
SUB = 8


def swapped(edge, axis, first, wrap):
    count = lax.axis_size(axis)
    pairs = [(i, (i + 1) % count) for i in range(first, count if wrap else count - 1, 2)]
    return lax.ppermute(edge, axis, pairs + [(j, i) for i, j in pairs])


def exchange(rows):
    return lax.all_to_all(rows, GROUP_AXES, split_axis=0, concat_axis=0, tiled=True)


def tile_row(y, half):
    return (y // SUB) * (2 * SUB) + half * SUB + y % SUB


def one_hot(index, size):
    place = lax.broadcasted_iota(jnp.int32, (size, index.shape[1]), 0)
    return (place == index).astype(jnp.bfloat16)


def log2(size):
    return size.bit_length() - 1


def dispatch_kernel(
    ny,
    nx,
    dest,
    slot,
    convect,
    state_hbm,
    slots,
    lat_even,
    lat_odd,
    lon_even,
    lon_odd,
    target,
    filled,
    state,
    chosen,
    choice,
    total,
    edges,
    arrived,
):
    load = pltpu.make_async_copy(state_hbm, state, arrived)
    load.start()
    width = state.shape[0] // (ny * 2)
    lanes = nx // 2
    lower = choice.shape[1]
    uppers = chosen.shape[2] // width
    depth = choice.shape[2]
    lines = depth // nx
    steps = ny // lines
    group = filled.shape[0]
    capacity = ny * nx // group
    shift, mask = log2(lower), lower - 1
    live = convect[...] > 0
    goal = jnp.where(live, dest[...] * capacity + slot[...], ny * nx)
    owner = goal >> log2(capacity)
    owners = lax.broadcasted_iota(jnp.int32, (group, nx), 0)
    counts = jnp.zeros((group, nx), jnp.int32)
    for y in range(ny):
        counts += (owners == owner[y : y + 1]).astype(jnp.int32)
    filled[...] = jnp.broadcast_to(jnp.sum(counts, axis=1, keepdims=True), filled.shape)
    for half in range(2):
        target[half] = goal[:, half * lanes : (half + 1) * lanes]
    goals = goal.T
    load.wait()

    def build(g, b):
        for line in range(lines):
            y = g * lines + line
            choice[b, :, pl.ds(line * nx, nx)] = one_hot(goal[y : y + 1] & mask, lower)
            upper = jnp.broadcast_to(goals[:, y : y + 1] >> shift, (nx, width))
            for half in range(2):
                part = slice(half * lanes, (half + 1) * lanes)
                values = state[pl.ds(tile_row(y, half), width, stride=2 * ny), :].T
                if half == 0:
                    edges[pl.ds(y, 1), :] = values[:1]
                else:
                    edges[pl.ds(ny + y, 1), :] = values[lanes - 1 :]
                values = values.astype(jnp.bfloat16)
                rows = pl.ds(line * nx + half * lanes, lanes)
                for h in range(uppers):
                    chosen[b, rows, pl.ds(h * width, width)] = jnp.where(
                        upper[part] == h, values, jnp.zeros_like(values)
                    )

    def multiply(g, b):
        product = jnp.dot(choice[b], chosen[b], preferred_element_type=jnp.float32)
        if g == 0:
            total[...] = product
        else:
            total[...] += product

    build(0, 0)
    for g in range(steps):
        if g < steps - 1:
            build(g + 1, (g + 1) % 2)
        multiply(g, g % 2)
    for h in range(uppers):
        slots[pl.ds(h * lower, lower), :] = total[:, pl.ds(h * width, width)].astype(slots.dtype)

    odd = lax.axis_index("lat") % 2 == 1
    for half in range(2):
        part = pl.ds(half * lanes, lanes)
        south = state[pl.ds(tile_row(0, half), width, stride=2 * ny), :]
        north = state[pl.ds(tile_row(ny - 1, half), width, stride=2 * ny), :]
        lat_even[:, part] = jnp.where(odd, south, north).astype(lat_even.dtype)
        lat_odd[:, part] = jnp.where(odd, north, south).astype(lat_odd.dtype)
    odd = lax.axis_index("span") == 1
    west, east = edges[pl.ds(0, ny), :], edges[pl.ds(ny, ny), :]
    lon_even[...] = jnp.where(odd, west, east).astype(lon_even.dtype)
    lon_odd[...] = jnp.where(odd, east, west).astype(lon_odd.dtype)


def dispatch(dest, slot, convect, state, group):
    ny, nx = dest.shape
    width, count = state.shape[0] // (ny * 2), ny * nx
    uppers, depth = 4, 4 * nx
    lower = count // uppers
    vmem = pl.BlockSpec(memory_space=pltpu.VMEM)
    kernel = lambda *refs: dispatch_kernel(ny, nx, *refs)
    shape = jax.ShapeDtypeStruct
    return pl.pallas_call(
        kernel,
        out_shape=(
            shape((count, width), jnp.bfloat16),
            shape((width, nx), jnp.bfloat16),
            shape((width, nx), jnp.bfloat16),
            shape((ny, width), jnp.bfloat16),
            shape((ny, width), jnp.bfloat16),
            shape((2, ny, nx // 2), jnp.int32),
            shape((group, width), jnp.int32),
        ),
        in_specs=[vmem, vmem, vmem, pl.BlockSpec(memory_space=pl.ANY)],
        out_specs=(vmem,) * 7,
        scratch_shapes=[
            pltpu.VMEM(state.shape, jnp.float32),
            pltpu.VMEM((2, depth, uppers * width), jnp.bfloat16),
            pltpu.VMEM((2, lower, depth), jnp.bfloat16),
            pltpu.VMEM((lower, uppers * width), jnp.float32),
            pltpu.VMEM((2 * ny, width), jnp.float32),
            pltpu.SemaphoreType.DMA,
        ],
        compiler_params=pltpu.CompilerParams(vmem_limit_bytes=63 * MIB),
        cost_estimate=pl.CostEstimate(
            flops=2 * count * count * width,
            bytes_accessed=6 * count * width,
            transcendentals=0,
        ),
        name="dispatch",
    )(dest, slot, convect, state)


def silu_of_half(half):
    return half + half * jnp.tanh(half)


def network_kernel(
    capacity,
    filled,
    columns,
    recalled,
    w_in,
    w_mid,
    w_deep,
    w_out,
    tend,
    renewed,
    half_in,
    half_mid,
    half_deep,
):
    @pl.when(pl.program_id(0) == 0)
    def _():
        for half, weights in ((half_in, w_in), (half_mid, w_mid), (half_deep, w_deep)):
            half[...] = weights[...] * jnp.bfloat16(0.5)

    width = columns.shape[1]
    size, wide = PART, w_in.shape[1]
    parts = columns.shape[0] // size
    rows = [pl.ds(p * size, size) for p in range(parts)]
    values = [[columns[r, :], recalled[r, :]] for r in rows]
    waiting = []

    def settle():
        sums, kept = waiting.pop(0)
        kept.append(silu_of_half(sums).astype(jnp.bfloat16))

    for weights in (half_in, half_mid, half_deep):
        following = [[] for _ in rows]
        for p in range(parts):
            joined = jnp.concatenate(values[p], axis=1)
            for n in range(weights.shape[1] // wide):
                piece = weights[:, pl.ds(n * wide, wide)]
                sums = jnp.dot(joined, piece, preferred_element_type=jnp.float32)
                waiting.append((sums, following[p]))
                if len(waiting) > 1:
                    settle()
        values = following
    settle()
    owners = size // capacity
    place = lax.broadcasted_iota(jnp.int32, (capacity, width), 0)
    for p in range(parts):
        joined = jnp.concatenate(values[p], axis=1)
        result = jnp.dot(joined, w_out[...], preferred_element_type=jnp.float32)
        tend[rows[p], :] = result[:, :width].astype(tend.dtype)
        for o in range(owners):
            part = pl.ds(p * size + o * capacity, capacity)
            live = place < filled[pl.ds(p * owners + o, 1), :]
            update = result[o * capacity : (o + 1) * capacity, width:]
            old = recalled[part, :].astype(jnp.float32)
            renewed[part, :] = (old + jnp.where(live, update, 0.0)).astype(renewed.dtype)


def network(filled, columns, recalled, w_in, w_mid, w_deep, w_out):
    count, width = columns.shape
    capacity = count // filled.shape[0]
    rows = pl.BlockSpec((ROWS_MLP, width), lambda i: (i, 0))
    counts = pl.BlockSpec((ROWS_MLP // capacity, width), lambda i: (i, 0))
    whole = lambda w: pl.BlockSpec(w.shape, lambda i: (0, 0))
    kernel = lambda *refs: network_kernel(capacity, *refs)
    weights = (w_in, w_mid, w_deep, w_out)
    return pl.pallas_call(
        kernel,
        grid=(count // ROWS_MLP,),
        out_shape=(
            jax.ShapeDtypeStruct((count, width), jnp.bfloat16),
            jax.ShapeDtypeStruct((count, width), jnp.bfloat16),
        ),
        in_specs=[counts, rows, rows] + [whole(w) for w in weights],
        out_specs=(rows, rows),
        scratch_shapes=[pltpu.VMEM(w.shape, w.dtype) for w in weights[:3]],
        compiler_params=pltpu.CompilerParams(vmem_limit_bytes=VMEM_LIMIT),
        cost_estimate=pl.CostEstimate(
            flops=2 * count * sum(w.size for w in weights),
            bytes_accessed=8 * count * width + 2 * sum(w.size for w in weights),
            transcendentals=count * 3 * w_mid.shape[0],
        ),
        name="network",
    )(filled, columns, recalled, *weights)


def finish_kernel(
    ny,
    nx,
    target,
    tend_hbm,
    state_hbm,
    winds_hbm,
    lat_even,
    lat_odd,
    lon_even,
    lon_odd,
    out_hbm,
    tend,
    state,
    winds,
    table,
    low,
    high,
    moved,
    flow,
    arrived,
    left_over,
):
    width = state.shape[0] // (ny * 2)
    lanes = nx // 2
    subs = ny // SUB
    levels = winds.shape[0] // (4 * ny)
    copies = [
        pltpu.make_async_copy(tend_hbm, tend, arrived.at[0]),
        pltpu.make_async_copy(state_hbm, state, arrived.at[1]),
        pltpu.make_async_copy(winds_hbm, winds, arrived.at[2]),
    ]
    for copy in copies:
        copy.start()
    odd = lax.axis_index("span") == 1
    evens, odds = lon_even[...].astype(jnp.float32), lon_odd[...].astype(jnp.float32)
    west = jnp.where(odd, evens, odds)
    east = jnp.where(odd, odds, evens)
    odd = lax.axis_index("lat") % 2 == 1
    for half in range(2):
        part = pl.ds(half * lanes, lanes)
        evens, odds = lat_even[:, part].astype(jnp.float32), lat_odd[:, part].astype(jnp.float32)
        low[half] = jnp.where(odd, evens, odds)
        high[half] = jnp.where(odd, odds, evens)
    lower = table.shape[1]
    uppers = table.shape[0] // width
    shift, mask = log2(lower), lower - 1
    copies[0].wait()
    for h in range(uppers):
        rows = tend[pl.ds(h * lower, lower), :].astype(jnp.float32)
        table[pl.ds(h * width, width), :] = rows.T.astype(table.dtype)

    lane = lax.broadcasted_iota(jnp.int32, (SUB, lanes), 1)
    line = lax.broadcasted_iota(jnp.int32, (SUB, lanes), 0)
    tiles = [(sub, half) for sub in range(subs) for half in range(2)]

    def block(r, sub, half):
        return pl.ds(r * (2 * ny) + (sub * 2 + half) * SUB, SUB)

    def move(y):
        index = jnp.concatenate([target[half, pl.ds(y, 1), :] for half in range(2)], axis=1)
        candidates = jnp.dot(
            table[...], one_hot(index & mask, lower), preferred_element_type=jnp.float32
        )
        upper = jnp.broadcast_to(index >> shift, (width, nx))
        change = jnp.zeros((width, nx), jnp.float32)
        for h in range(uppers):
            change = jnp.where(upper == h, candidates[h * width : (h + 1) * width], change)
        for half in range(2):
            place = pl.ds(tile_row(y, half), width, stride=2 * ny)
            moved[place, :] = change[:, half * lanes : (half + 1) * lanes]

    def advect(k):
        zonal = {t: winds[block(k, *t), :] for t in tiles}
        meridional = {t: winds[block(levels + k, *t), :] for t in tiles}
        for f in range(width // levels):
            r = f * levels + k
            s = {t: state[block(r, *t), :] for t in tiles}
            first = pltpu.roll(west, (width - r) % width, axis=1)
            last = pltpu.roll(east, width - 1 - r, axis=1)
            up = {t: pltpu.roll(s[t], 1, axis=1) for t in tiles}
            down = {t: pltpu.roll(s[t], lanes - 1, axis=1) for t in tiles}
            rise = {t: pltpu.roll(s[t], 1, axis=0) for t in tiles}
            fall = {t: pltpu.roll(s[t], SUB - 1, axis=0) for t in tiles}
            for sub, half in tiles:
                t = (sub, half)
                edge = slice(sub * SUB, (sub + 1) * SUB)
                left = jnp.where(lane == 0, up[sub, 0] if half else first[edge], up[t])
                right = jnp.where(lane == lanes - 1, last[edge] if half else down[sub, 1], down[t])
                under = rise[sub - 1, half] if sub else low[half, pl.ds(r, 1), :]
                over = fall[sub + 1, half] if sub < subs - 1 else high[half, pl.ds(r, 1), :]
                below = jnp.where(line == 0, under, rise[t])
                above = jnp.where(line == SUB - 1, over, fall[t])
                flow[block(r, *t), :] = (
                    s[t]
                    - jnp.maximum(zonal[t], 0.0) * (s[t] - left)
                    - jnp.minimum(zonal[t], 0.0) * (right - s[t])
                    - jnp.maximum(meridional[t], 0.0) * (s[t] - below)
                    - jnp.minimum(meridional[t], 0.0) * (above - s[t])
                )

    ahead = 2
    share = levels // (ny - ahead) + 1
    for y in range(ny):
        move(y)
        if y == ahead - 1:
            copies[1].wait()
            copies[2].wait()
        start = (y - ahead) * share
        for k in range(max(start, 0), max(min(start + share, levels), 0)):
            advect(k)
    pieces = left_over.shape[0]
    size = state.shape[0] // pieces
    sends = []
    for p in range(pieces):
        rows = pl.ds(p * size, size)
        flow[rows, :] = flow[rows, :] + moved[rows, :]
        sends.append(pltpu.make_async_copy(flow.at[rows, :], out_hbm.at[rows, :], left_over.at[p]))
        sends[-1].start()
    for send in sends:
        send.wait()


def finish(target, tend, state, winds, *edges):
    _, ny, lanes = target.shape
    nx = 2 * lanes
    count, width = tend.shape
    uppers = 8
    vmem = pl.BlockSpec(memory_space=pltpu.VMEM)
    hbm = pl.BlockSpec(memory_space=pl.ANY)
    kernel = lambda *refs: finish_kernel(ny, nx, *refs)
    return pl.pallas_call(
        kernel,
        out_shape=jax.ShapeDtypeStruct(state.shape, jnp.float32),
        in_specs=[vmem, hbm, hbm, hbm, vmem, vmem, vmem, vmem],
        out_specs=hbm,
        scratch_shapes=[
            pltpu.VMEM(tend.shape, tend.dtype),
            pltpu.VMEM(state.shape, jnp.float32),
            pltpu.VMEM(winds.shape, jnp.float32),
            pltpu.VMEM((uppers * width, count // uppers), jnp.bfloat16),
            pltpu.VMEM((2, width, lanes), jnp.float32),
            pltpu.VMEM((2, width, lanes), jnp.float32),
            pltpu.VMEM(state.shape, jnp.float32),
            pltpu.VMEM(state.shape, jnp.float32),
            pltpu.SemaphoreType.DMA((3,)),
            pltpu.SemaphoreType.DMA((4,)),
        ],
        compiler_params=pltpu.CompilerParams(vmem_limit_bytes=VMEM_LIMIT),
        cost_estimate=pl.CostEstimate(
            flops=2 * count * count * width,
            bytes_accessed=14 * count * width,
            transcendentals=0,
        ),
        name="finish",
    )(target, tend, state, winds, *edges)


def to_tiles(field):
    fields, levels, ny, nx = field.shape
    tiles = field.reshape(fields * levels, ny // SUB, SUB, 2, nx // 2)
    return tiles.transpose(0, 1, 3, 2, 4).reshape(fields * levels * ny * 2, nx // 2)


def from_tiles(tiles, shape):
    fields, levels, ny, nx = shape
    field = tiles.reshape(fields * levels, ny // SUB, 2, SUB, nx // 2)
    return field.transpose(0, 1, 3, 2, 4).reshape(shape)


def body(state, winds, memory, w_in, w_mid, w_deep, w_out, dest, slot, convect):
    group = lax.axis_size(GROUP_AXES)

    recalled = exchange(memory)
    flat_state, flat_winds = to_tiles(state), to_tiles(winds)
    columns, lat_even, lat_odd, lon_even, lon_odd, target, filled = dispatch(
        dest, slot, convect, flat_state, group
    )
    loop = ("lon", "span")
    lon_even = swapped(lon_even, loop, 0, True)
    lon_odd = swapped(lon_odd, loop, 1, True)
    lat_even = swapped(lat_even, "lat", 0, False)
    lat_odd = swapped(lat_odd, "lat", 1, False)
    tend, renewed = network(filled, columns, recalled, w_in, w_mid, w_deep, w_out)
    edges = (lat_even, lat_odd, lon_even)
    renewed, edges = lax.optimization_barrier((renewed, edges))
    new_memory = exchange(renewed)
    new_state = finish(target, tend, flat_state, flat_winds, *edges, lon_odd)
    return from_tiles(new_state, state.shape), new_memory


def solution(mesh):
    field = P(None, None, "lat", ("lon", "span"))
    slots = P(("lon", "lat", "span"), None)
    plane = P("lat", ("lon", "span"))
    in_specs = (field, field, slots, P(), P(), P(), P(), plane, plane, plane)
    return jax.shard_map(
        body, mesh=mesh, in_specs=in_specs, out_specs=(field, slots), check_vma=False
    )
```

```python
import jax
import jax.numpy as jnp
from jax import lax
from jax.experimental import pallas as pl
from jax.experimental.pallas import tpu as pltpu
from jax.sharding import PartitionSpec as P

GROUP_AXES = ("lat", "span")
MIB = 1024 * 1024
ROWS_MLP = 2048
PART = 1024
VMEM_LIMIT = 60 * MIB
SUB = 8


def swapped(edge, axis, first, wrap):
    count = lax.axis_size(axis)
    pairs = [(i, (i + 1) % count) for i in range(first, count if wrap else count - 1, 2)]
    return lax.ppermute(edge, axis, pairs + [(j, i) for i, j in pairs])


def exchange(rows):
    return lax.all_to_all(rows, GROUP_AXES, split_axis=0, concat_axis=0, tiled=True)


def tile_row(y, half):
    return (y // SUB) * (2 * SUB) + half * SUB + y % SUB


def one_hot(index, size):
    lanes = index.shape[1]
    step = 2 * SUB
    index = jnp.broadcast_to(index, (step, lanes)).astype(jnp.int16)
    place = lax.broadcasted_iota(jnp.int32, (step, lanes), 0).astype(jnp.int16)
    one, zero = jnp.ones((step, lanes), jnp.bfloat16), jnp.zeros((step, lanes), jnp.bfloat16)
    blocks = [
        jnp.where(index == place + jnp.int16(start), one, zero) for start in range(0, size, step)
    ]
    return jnp.concatenate(blocks, axis=0)


def log2(size):
    return size.bit_length() - 1


def dispatch_kernel(
    ny,
    nx,
    dest,
    slot,
    convect,
    state_hbm,
    slots,
    lat_even,
    lat_odd,
    lon_even,
    lon_odd,
    target,
    filled,
    state,
    chosen,
    choice,
    total,
    edges,
    arrived,
):
    load = pltpu.make_async_copy(state_hbm, state, arrived)
    load.start()
    width = state.shape[0] // (ny * 2)
    lanes = nx // 2
    lower = choice.shape[1]
    uppers = chosen.shape[2] // width
    depth = choice.shape[2]
    lines = depth // nx
    steps = ny // lines
    group = filled.shape[0]
    capacity = ny * nx // group
    shift, mask = log2(lower), lower - 1
    live = convect[...] > 0
    goal = jnp.where(live, dest[...] * capacity + slot[...], ny * nx)
    owner = goal >> log2(capacity)
    owners = lax.broadcasted_iota(jnp.int32, (group, nx), 0)
    counts = jnp.zeros((group, nx), jnp.int32)
    for y in range(ny):
        counts += (owners == owner[y : y + 1]).astype(jnp.int32)
    filled[...] = jnp.broadcast_to(jnp.sum(counts, axis=1, keepdims=True), filled.shape)
    for half in range(2):
        target[half] = goal[:, half * lanes : (half + 1) * lanes]
    goals = goal.T
    load.wait()

    def build(g, b):
        for line in range(lines):
            y = g * lines + line
            choice[b, :, pl.ds(line * nx, nx)] = one_hot(goal[y : y + 1] & mask, lower)
            upper = jnp.broadcast_to(goals[:, y : y + 1] >> shift, (nx, width)).astype(jnp.int16)
            for half in range(2):
                part = slice(half * lanes, (half + 1) * lanes)
                values = state[pl.ds(tile_row(y, half), width, stride=2 * ny), :].T
                if half == 0:
                    edges[pl.ds(y, 1), :] = values[:1]
                else:
                    edges[pl.ds(ny + y, 1), :] = values[lanes - 1 :]
                values = values.astype(jnp.bfloat16)
                rows = pl.ds(line * nx + half * lanes, lanes)
                for h in range(uppers):
                    chosen[b, rows, pl.ds(h * width, width)] = jnp.where(
                        upper[part] == h, values, jnp.zeros_like(values)
                    )

    def multiply(g, b):
        product = jnp.dot(choice[b], chosen[b], preferred_element_type=jnp.float32)
        if g == 0:
            total[...] = product
        else:
            total[...] += product

    build(0, 0)
    for g in range(steps):
        if g < steps - 1:
            build(g + 1, (g + 1) % 2)
        multiply(g, g % 2)
    for h in range(uppers):
        slots[pl.ds(h * lower, lower), :] = total[:, pl.ds(h * width, width)].astype(slots.dtype)

    odd = lax.axis_index("lat") % 2 == 1
    for half in range(2):
        part = pl.ds(half * lanes, lanes)
        south = state[pl.ds(tile_row(0, half), width, stride=2 * ny), :]
        north = state[pl.ds(tile_row(ny - 1, half), width, stride=2 * ny), :]
        lat_even[:, part] = jnp.where(odd, south, north).astype(lat_even.dtype)
        lat_odd[:, part] = jnp.where(odd, north, south).astype(lat_odd.dtype)
    odd = lax.axis_index("span") == 1
    west, east = edges[pl.ds(0, ny), :], edges[pl.ds(ny, ny), :]
    lon_even[...] = jnp.where(odd, west, east).astype(lon_even.dtype)
    lon_odd[...] = jnp.where(odd, east, west).astype(lon_odd.dtype)


def dispatch(dest, slot, convect, state, group):
    ny, nx = dest.shape
    width, count = state.shape[0] // (ny * 2), ny * nx
    uppers, depth = 4, 4 * nx
    lower = count // uppers
    vmem = pl.BlockSpec(memory_space=pltpu.VMEM)
    kernel = lambda *refs: dispatch_kernel(ny, nx, *refs)
    shape = jax.ShapeDtypeStruct
    return pl.pallas_call(
        kernel,
        out_shape=(
            shape((count, width), jnp.bfloat16),
            shape((width, nx), jnp.bfloat16),
            shape((width, nx), jnp.bfloat16),
            shape((ny, width), jnp.bfloat16),
            shape((ny, width), jnp.bfloat16),
            shape((2, ny, nx // 2), jnp.int32),
            shape((group, width), jnp.int32),
        ),
        in_specs=[vmem, vmem, vmem, pl.BlockSpec(memory_space=pl.ANY)],
        out_specs=(vmem,) * 7,
        scratch_shapes=[
            pltpu.VMEM(state.shape, jnp.float32),
            pltpu.VMEM((2, depth, uppers * width), jnp.bfloat16),
            pltpu.VMEM((2, lower, depth), jnp.bfloat16),
            pltpu.VMEM((lower, uppers * width), jnp.float32),
            pltpu.VMEM((2 * ny, width), jnp.float32),
            pltpu.SemaphoreType.DMA,
        ],
        compiler_params=pltpu.CompilerParams(vmem_limit_bytes=63 * MIB),
        cost_estimate=pl.CostEstimate(
            flops=2 * count * count * width,
            bytes_accessed=6 * count * width,
            transcendentals=0,
        ),
        name="dispatch",
    )(dest, slot, convect, state)


def silu_of_half(half):
    return half + half * jnp.tanh(half)


def network_kernel(
    capacity,
    filled,
    columns,
    recalled,
    w_in,
    w_mid,
    w_deep,
    w_out,
    tend,
    renewed,
    half_in,
    half_mid,
    half_deep,
):
    @pl.when(pl.program_id(0) == 0)
    def _():
        for half, weights in ((half_in, w_in), (half_mid, w_mid), (half_deep, w_deep)):
            half[...] = weights[...] * jnp.bfloat16(0.5)

    width = columns.shape[1]
    size, wide = PART, w_in.shape[1]
    parts = columns.shape[0] // size
    rows = [pl.ds(p * size, size) for p in range(parts)]
    values = [[columns[r, :], recalled[r, :]] for r in rows]
    waiting = []

    def settle():
        sums, kept = waiting.pop(0)
        kept.append(silu_of_half(sums).astype(jnp.bfloat16))

    for weights in (half_in, half_mid, half_deep):
        following = [[] for _ in rows]
        for p in range(parts):
            joined = jnp.concatenate(values[p], axis=1)
            for n in range(weights.shape[1] // wide):
                piece = weights[:, pl.ds(n * wide, wide)]
                sums = jnp.dot(joined, piece, preferred_element_type=jnp.float32)
                waiting.append((sums, following[p]))
                if len(waiting) > 1:
                    settle()
        values = following
    settle()
    owners = size // capacity
    place = lax.broadcasted_iota(jnp.int32, (capacity, width), 0)
    for p in range(parts):
        joined = jnp.concatenate(values[p], axis=1)
        result = jnp.dot(joined, w_out[...], preferred_element_type=jnp.float32)
        tend[rows[p], :] = result[:, :width].astype(tend.dtype)
        for o in range(owners):
            part = pl.ds(p * size + o * capacity, capacity)
            live = place < filled[pl.ds(p * owners + o, 1), :]
            update = result[o * capacity : (o + 1) * capacity, width:]
            old = recalled[part, :].astype(jnp.float32)
            renewed[part, :] = (old + jnp.where(live, update, 0.0)).astype(renewed.dtype)


def network(filled, columns, recalled, w_in, w_mid, w_deep, w_out):
    count, width = columns.shape
    capacity = count // filled.shape[0]
    rows = pl.BlockSpec((ROWS_MLP, width), lambda i: (i, 0))
    counts = pl.BlockSpec((ROWS_MLP // capacity, width), lambda i: (i, 0))
    whole = lambda w: pl.BlockSpec(w.shape, lambda i: (0, 0))
    kernel = lambda *refs: network_kernel(capacity, *refs)
    weights = (w_in, w_mid, w_deep, w_out)
    return pl.pallas_call(
        kernel,
        grid=(count // ROWS_MLP,),
        out_shape=(
            jax.ShapeDtypeStruct((count, width), jnp.bfloat16),
            jax.ShapeDtypeStruct((count, width), jnp.bfloat16),
        ),
        in_specs=[counts, rows, rows] + [whole(w) for w in weights],
        out_specs=(rows, rows),
        scratch_shapes=[pltpu.VMEM(w.shape, w.dtype) for w in weights[:3]],
        compiler_params=pltpu.CompilerParams(vmem_limit_bytes=VMEM_LIMIT),
        cost_estimate=pl.CostEstimate(
            flops=2 * count * sum(w.size for w in weights),
            bytes_accessed=8 * count * width + 2 * sum(w.size for w in weights),
            transcendentals=count * 3 * w_mid.shape[0],
        ),
        name="network",
    )(filled, columns, recalled, *weights)


def finish_kernel(
    ny,
    nx,
    target,
    tend_hbm,
    state_hbm,
    winds_hbm,
    lat_even,
    lat_odd,
    lon_even,
    lon_odd,
    out_hbm,
    tend,
    state,
    winds,
    table,
    low,
    high,
    moved,
    flow,
    arrived,
    left_over,
):
    width = state.shape[0] // (ny * 2)
    lanes = nx // 2
    subs = ny // SUB
    levels = winds.shape[0] // (4 * ny)
    count = ny * nx
    copies = [
        pltpu.make_async_copy(tend_hbm, tend, arrived.at[0]),
        pltpu.make_async_copy(state_hbm, state, arrived.at[1]),
        pltpu.make_async_copy(winds_hbm, winds, arrived.at[2]),
    ]
    for copy in copies:
        copy.start()
    odd = lax.axis_index("span") == 1
    evens, odds = lon_even[...].astype(jnp.float32), lon_odd[...].astype(jnp.float32)
    west = jnp.where(odd, evens, odds)
    east = jnp.where(odd, odds, evens)
    odd = lax.axis_index("lat") % 2 == 1
    for half in range(2):
        part = pl.ds(half * lanes, lanes)
        evens, odds = lat_even[:, part].astype(jnp.float32), lat_odd[:, part].astype(jnp.float32)
        low[half] = jnp.where(odd, evens, odds)
        high[half] = jnp.where(odd, odds, evens)
    lower = table.shape[1]
    uppers = table.shape[0] // width
    shift, mask = log2(lower), lower - 1
    copies[0].wait()
    for h in range(uppers):
        rows = tend[pl.ds(h * lower, lower), :].astype(jnp.float32)
        table[pl.ds(h * width, width), :] = rows.T.astype(table.dtype)

    lane = lax.broadcasted_iota(jnp.int32, (SUB, lanes), 1)
    line = lax.broadcasted_iota(jnp.int32, (SUB, lanes), 0)
    tiles = [(sub, half) for sub in range(subs) for half in range(2)]

    def block(r, sub, half):
        return pl.ds(r * (2 * ny) + (sub * 2 + half) * SUB, SUB)

    def move(y):
        index = jnp.concatenate([target[half, pl.ds(y, 1), :] for half in range(2)], axis=1)
        wanted = jnp.where(index == count, -1, index & mask)
        candidates = jnp.dot(
            table[...], one_hot(wanted, lower), preferred_element_type=jnp.float32
        ).reshape(uppers, width // SUB, SUB, nx)
        upper = jnp.broadcast_to(index >> shift, (SUB, nx))
        change = candidates[0]
        for h in range(1, uppers):
            change = jnp.where((upper == h)[None], candidates[h], change)
        change = change.reshape(width, nx)
        for half in range(2):
            place = pl.ds(tile_row(y, half), width, stride=2 * ny)
            moved[place, :] = change[:, half * lanes : (half + 1) * lanes]

    def advect(k):
        zonal = {t: winds[block(k, *t), :] for t in tiles}
        meridional = {t: winds[block(levels + k, *t), :] for t in tiles}
        for f in range(width // levels):
            r = f * levels + k
            s = {t: state[block(r, *t), :] for t in tiles}
            first = pltpu.roll(west, (width - r) % width, axis=1)
            last = pltpu.roll(east, width - 1 - r, axis=1)
            up = {t: pltpu.roll(s[t], 1, axis=1) for t in tiles}
            down = {t: pltpu.roll(s[t], lanes - 1, axis=1) for t in tiles}
            rise = {t: pltpu.roll(s[t], 1, axis=0) for t in tiles}
            fall = {t: pltpu.roll(s[t], SUB - 1, axis=0) for t in tiles}
            for sub, half in tiles:
                t = (sub, half)
                edge = slice(sub * SUB, (sub + 1) * SUB)
                left = jnp.where(lane == 0, up[sub, 0] if half else first[edge], up[t])
                right = jnp.where(lane == lanes - 1, last[edge] if half else down[sub, 1], down[t])
                under = rise[sub - 1, half] if sub else low[half, pl.ds(r, 1), :]
                over = fall[sub + 1, half] if sub < subs - 1 else high[half, pl.ds(r, 1), :]
                below = jnp.where(line == 0, under, rise[t])
                above = jnp.where(line == SUB - 1, over, fall[t])
                flow[block(r, *t), :] = (
                    s[t]
                    - jnp.maximum(zonal[t], 0.0) * (s[t] - left)
                    - jnp.minimum(zonal[t], 0.0) * (right - s[t])
                    - jnp.maximum(meridional[t], 0.0) * (s[t] - below)
                    - jnp.minimum(meridional[t], 0.0) * (above - s[t])
                )

    ahead = 2
    share = levels // (ny - ahead) + 1
    for y in range(ny):
        move(y)
        if y == ahead - 1:
            copies[1].wait()
            copies[2].wait()
        start = (y - ahead) * share
        for k in range(max(start, 0), max(min(start + share, levels), 0)):
            advect(k)
    pieces = left_over.shape[0]
    size = state.shape[0] // pieces
    sends = []
    for p in range(pieces):
        rows = pl.ds(p * size, size)
        flow[rows, :] = flow[rows, :] + moved[rows, :]
        sends.append(pltpu.make_async_copy(flow.at[rows, :], out_hbm.at[rows, :], left_over.at[p]))
        sends[-1].start()
    for send in sends:
        send.wait()


def finish(target, tend, state, winds, *edges):
    _, ny, lanes = target.shape
    nx = 2 * lanes
    count, width = tend.shape
    uppers = 8
    vmem = pl.BlockSpec(memory_space=pltpu.VMEM)
    hbm = pl.BlockSpec(memory_space=pl.ANY)
    kernel = lambda *refs: finish_kernel(ny, nx, *refs)
    return pl.pallas_call(
        kernel,
        out_shape=jax.ShapeDtypeStruct(state.shape, jnp.float32),
        in_specs=[vmem, hbm, hbm, hbm, vmem, vmem, vmem, vmem],
        out_specs=hbm,
        scratch_shapes=[
            pltpu.VMEM(tend.shape, tend.dtype),
            pltpu.VMEM(state.shape, jnp.float32),
            pltpu.VMEM(winds.shape, jnp.float32),
            pltpu.VMEM((uppers * width, count // uppers), jnp.bfloat16),
            pltpu.VMEM((2, width, lanes), jnp.float32),
            pltpu.VMEM((2, width, lanes), jnp.float32),
            pltpu.VMEM(state.shape, jnp.float32),
            pltpu.VMEM(state.shape, jnp.float32),
            pltpu.SemaphoreType.DMA((3,)),
            pltpu.SemaphoreType.DMA((4,)),
        ],
        compiler_params=pltpu.CompilerParams(vmem_limit_bytes=VMEM_LIMIT),
        cost_estimate=pl.CostEstimate(
            flops=2 * count * count * width,
            bytes_accessed=14 * count * width,
            transcendentals=0,
        ),
        name="finish",
    )(target, tend, state, winds, *edges)


def to_tiles(field):
    fields, levels, ny, nx = field.shape
    tiles = field.reshape(fields * levels, ny // SUB, SUB, 2, nx // 2)
    return tiles.transpose(0, 1, 3, 2, 4).reshape(fields * levels * ny * 2, nx // 2)


def from_tiles(tiles, shape):
    fields, levels, ny, nx = shape
    field = tiles.reshape(fields * levels, ny // SUB, 2, SUB, nx // 2)
    return field.transpose(0, 1, 3, 2, 4).reshape(shape)


def body(state, winds, memory, w_in, w_mid, w_deep, w_out, dest, slot, convect):
    group = lax.axis_size(GROUP_AXES)

    recalled = exchange(memory)
    flat_state, flat_winds = to_tiles(state), to_tiles(winds)
    columns, lat_even, lat_odd, lon_even, lon_odd, target, filled = dispatch(
        dest, slot, convect, flat_state, group
    )
    loop = ("lon", "span")
    lon_even = swapped(lon_even, loop, 0, True)
    lon_odd = swapped(lon_odd, loop, 1, True)
    lat_even = swapped(lat_even, "lat", 0, False)
    lat_odd = swapped(lat_odd, "lat", 1, False)
    tend, renewed = network(filled, columns, recalled, w_in, w_mid, w_deep, w_out)
    edges = (lat_even, lat_odd, lon_even)
    renewed, edges = lax.optimization_barrier((renewed, edges))
    new_memory = exchange(renewed)
    new_state = finish(target, tend, flat_state, flat_winds, *edges, lon_odd)
    return from_tiles(new_state, state.shape), new_memory


def solution(mesh):
    field = P(None, None, "lat", ("lon", "span"))
    slots = P(("lon", "lat", "span"), None)
    plane = P("lat", ("lon", "span"))
    in_specs = (field, field, slots, P(), P(), P(), P(), plane, plane, plane)
    return jax.shard_map(
        body, mesh=mesh, in_specs=in_specs, out_specs=(field, slots), check_vma=False
    )
```

```python
import jax
import jax.numpy as jnp
from jax import lax
from jax.experimental import pallas as pl
from jax.experimental.pallas import tpu as pltpu
from jax.sharding import PartitionSpec as P

GROUP_AXES = ("lat", "span")
MIB = 1024 * 1024
ROWS_MLP = 2048
PART = 1024
VMEM_LIMIT = 60 * MIB
SUB = 8


def swapped(edge, axis, first, wrap):
    count = lax.axis_size(axis)
    pairs = [(i, (i + 1) % count) for i in range(first, count if wrap else count - 1, 2)]
    return lax.ppermute(edge, axis, pairs + [(j, i) for i, j in pairs])


def exchange(rows):
    return lax.all_to_all(rows, GROUP_AXES, split_axis=0, concat_axis=0, tiled=True)


def tile_row(y, half):
    return (y // SUB) * (2 * SUB) + half * SUB + y % SUB


def one_hot(index, size):
    lanes = index.shape[1]
    step = 2 * SUB
    index = jnp.broadcast_to(index, (step, lanes)).astype(jnp.int16)
    place = lax.broadcasted_iota(jnp.int32, (step, lanes), 0).astype(jnp.int16)
    one, zero = jnp.ones((step, lanes), jnp.bfloat16), jnp.zeros((step, lanes), jnp.bfloat16)
    blocks = [
        jnp.where(index == place + jnp.int16(start), one, zero) for start in range(0, size, step)
    ]
    return jnp.concatenate(blocks, axis=0)


def log2(size):
    return size.bit_length() - 1


def advect_level(ny, nx, state, winds, flow, k):
    lanes, subs = nx // 2, ny // SUB
    levels = winds.shape[0] // (4 * ny)
    lane = lax.broadcasted_iota(jnp.int32, (SUB, lanes), 1)
    line = lax.broadcasted_iota(jnp.int32, (SUB, lanes), 0)
    tiles = [(sub, half) for sub in range(subs) for half in range(2)]

    def block(r, sub, half):
        return pl.ds(r * (2 * ny) + (sub * 2 + half) * SUB, SUB)

    zonal = {t: winds[block(k, *t), :] for t in tiles}
    meridional = {t: winds[block(levels + k, *t), :] for t in tiles}
    for r in range(k, state.shape[0] // (2 * ny), levels):
        s = {t: state[block(r, *t), :] for t in tiles}
        up = {t: pltpu.roll(s[t], 1, axis=1) for t in tiles}
        down = {t: pltpu.roll(s[t], lanes - 1, axis=1) for t in tiles}
        rise = {t: pltpu.roll(s[t], 1, axis=0) for t in tiles}
        fall = {t: pltpu.roll(s[t], SUB - 1, axis=0) for t in tiles}
        for sub, half in tiles:
            t = (sub, half)
            left = jnp.where(lane == 0, up[sub, 0] if half else 0.0, up[t])
            right = jnp.where(lane == lanes - 1, 0.0 if half else down[sub, 1], down[t])
            below = jnp.where(line == 0, rise[sub - 1, half] if sub else 0.0, rise[t])
            above = jnp.where(
                line == SUB - 1, fall[sub + 1, half] if sub < subs - 1 else 0.0, fall[t]
            )
            flow[block(r, *t), :] = (
                s[t]
                - jnp.maximum(zonal[t], 0.0) * (s[t] - left)
                - jnp.minimum(zonal[t], 0.0) * (right - s[t])
                - jnp.maximum(meridional[t], 0.0) * (s[t] - below)
                - jnp.minimum(meridional[t], 0.0) * (above - s[t])
            )


def dispatch_kernel(
    ny,
    nx,
    dest,
    slot,
    convect,
    state_hbm,
    winds_hbm,
    slots,
    lat_even,
    lat_odd,
    lon_even,
    lon_odd,
    target,
    filled,
    flow_hbm,
    state,
    winds,
    flow,
    chosen,
    choice,
    total,
    edges,
    arrived,
    left_over,
):
    load = pltpu.make_async_copy(state_hbm, state, arrived.at[0])
    load.start()
    load_winds = pltpu.make_async_copy(winds_hbm, winds, arrived.at[1])
    load_winds.start()
    width = state.shape[0] // (ny * 2)
    lanes = nx // 2
    lower = choice.shape[1]
    uppers = chosen.shape[2] // width
    depth = choice.shape[2]
    lines = depth // nx
    steps = ny // lines
    group = filled.shape[0]
    capacity = ny * nx // group
    shift, mask = log2(lower), lower - 1
    live = convect[...] > 0
    goal = jnp.where(live, dest[...] * capacity + slot[...], ny * nx)
    owner = goal >> log2(capacity)
    owners = lax.broadcasted_iota(jnp.int32, (group, nx), 0)
    counts = jnp.zeros((group, nx), jnp.int32)
    for y in range(ny):
        counts += (owners == owner[y : y + 1]).astype(jnp.int32)
    filled[...] = jnp.broadcast_to(jnp.sum(counts, axis=1, keepdims=True), filled.shape)
    for half in range(2):
        target[half] = goal[:, half * lanes : (half + 1) * lanes]
    goals = goal.T
    load.wait()

    def build(g, b):
        for line in range(lines):
            y = g * lines + line
            choice[b, :, pl.ds(line * nx, nx)] = one_hot(goal[y : y + 1] & mask, lower)
            upper = jnp.broadcast_to(goals[:, y : y + 1] >> shift, (nx, width)).astype(jnp.int16)
            for half in range(2):
                part = slice(half * lanes, (half + 1) * lanes)
                values = state[pl.ds(tile_row(y, half), width, stride=2 * ny), :].T
                if half == 0:
                    edges[pl.ds(y, 1), :] = values[:1]
                else:
                    edges[pl.ds(ny + y, 1), :] = values[lanes - 1 :]
                values = values.astype(jnp.bfloat16)
                rows = pl.ds(line * nx + half * lanes, lanes)
                for h in range(uppers):
                    chosen[b, rows, pl.ds(h * width, width)] = jnp.where(
                        upper[part] == h, values, jnp.zeros_like(values)
                    )

    def multiply(g, b):
        product = jnp.dot(choice[b], chosen[b], preferred_element_type=jnp.float32)
        if g == 0:
            total[...] = product
        else:
            total[...] += product

    levels = winds.shape[0] // (4 * ny)
    share = levels // steps
    sends = []
    build(0, 0)
    for g in range(steps):
        if g < steps - 1:
            build(g + 1, (g + 1) % 2)
        multiply(g, g % 2)
        if g == 0:
            load_winds.wait()
        for k in range(g * share, (g + 1) * share):
            advect_level(ny, nx, state, winds, flow, k)
        for f in range(width // levels):
            rows = pl.ds((f * levels + g * share) * 2 * ny, share * 2 * ny)
            sends.append(
                pltpu.make_async_copy(flow.at[rows, :], flow_hbm.at[rows, :], left_over.at[g, f])
            )
            sends[-1].start()
    for h in range(uppers):
        slots[pl.ds(h * lower, lower), :] = total[:, pl.ds(h * width, width)].astype(slots.dtype)

    odd = lax.axis_index("lat") % 2 == 1
    for half in range(2):
        part = pl.ds(half * lanes, lanes)
        south = state[pl.ds(tile_row(0, half), width, stride=2 * ny), :]
        north = state[pl.ds(tile_row(ny - 1, half), width, stride=2 * ny), :]
        lat_even[:, part] = jnp.where(odd, south, north).astype(lat_even.dtype)
        lat_odd[:, part] = jnp.where(odd, north, south).astype(lat_odd.dtype)
    odd = lax.axis_index("span") == 1
    west, east = edges[pl.ds(0, ny), :], edges[pl.ds(ny, ny), :]
    lon_even[...] = jnp.where(odd, west, east).astype(lon_even.dtype)
    lon_odd[...] = jnp.where(odd, east, west).astype(lon_odd.dtype)
    for send in sends:
        send.wait()


def dispatch(dest, slot, convect, state, winds, group):
    ny, nx = dest.shape
    width, count = state.shape[0] // (ny * 2), ny * nx
    uppers, depth = 4, 4 * nx
    lower = count // uppers
    hbm = pl.BlockSpec(memory_space=pl.ANY)
    vmem = pl.BlockSpec(memory_space=pltpu.VMEM)
    kernel = lambda *refs: dispatch_kernel(ny, nx, *refs)
    shape = jax.ShapeDtypeStruct
    return pl.pallas_call(
        kernel,
        out_shape=(
            shape((count, width), jnp.bfloat16),
            shape((width, nx), jnp.bfloat16),
            shape((width, nx), jnp.bfloat16),
            shape((ny, width), jnp.bfloat16),
            shape((ny, width), jnp.bfloat16),
            shape((2, ny, nx // 2), jnp.int32),
            shape((group, width), jnp.int32),
            shape(state.shape, jnp.float32),
        ),
        in_specs=[vmem, vmem, vmem, hbm, hbm],
        out_specs=(vmem,) * 7 + (hbm,),
        scratch_shapes=[
            pltpu.VMEM(state.shape, jnp.float32),
            pltpu.VMEM(winds.shape, jnp.float32),
            pltpu.VMEM(state.shape, jnp.float32),
            pltpu.VMEM((2, depth, uppers * width), jnp.bfloat16),
            pltpu.VMEM((2, lower, depth), jnp.bfloat16),
            pltpu.VMEM((lower, uppers * width), jnp.float32),
            pltpu.VMEM((2 * ny, width), jnp.float32),
            pltpu.SemaphoreType.DMA((2,)),
            pltpu.SemaphoreType.DMA((4, 2)),
        ],
        compiler_params=pltpu.CompilerParams(vmem_limit_bytes=63 * MIB),
        cost_estimate=pl.CostEstimate(
            flops=2 * count * count * width,
            bytes_accessed=6 * count * width,
            transcendentals=0,
        ),
        name="dispatch",
    )(dest, slot, convect, state, winds)


def silu_of_half(half):
    return half + half * jnp.tanh(half)


def network_kernel(
    capacity,
    filled,
    columns,
    recalled,
    w_in,
    w_mid,
    w_deep,
    w_out,
    tend,
    renewed,
    half_in,
    half_mid,
    half_deep,
):
    @pl.when(pl.program_id(0) == 0)
    def _():
        for half, weights in ((half_in, w_in), (half_mid, w_mid), (half_deep, w_deep)):
            half[...] = weights[...] * jnp.bfloat16(0.5)

    width = columns.shape[1]
    size, wide = PART, w_in.shape[1]
    parts = columns.shape[0] // size
    rows = [pl.ds(p * size, size) for p in range(parts)]
    values = [[columns[r, :], recalled[r, :]] for r in rows]
    waiting = []

    def settle():
        sums, kept = waiting.pop(0)
        kept.append(silu_of_half(sums).astype(jnp.bfloat16))

    for weights in (half_in, half_mid, half_deep):
        following = [[] for _ in rows]
        for p in range(parts):
            joined = jnp.concatenate(values[p], axis=1)
            for n in range(weights.shape[1] // wide):
                piece = weights[:, pl.ds(n * wide, wide)]
                sums = jnp.dot(joined, piece, preferred_element_type=jnp.float32)
                waiting.append((sums, following[p]))
                if len(waiting) > 1:
                    settle()
        values = following
    settle()
    owners = size // capacity
    place = lax.broadcasted_iota(jnp.int32, (capacity, width), 0)
    for p in range(parts):
        joined = jnp.concatenate(values[p], axis=1)
        result = jnp.dot(joined, w_out[...], preferred_element_type=jnp.float32)
        tend[rows[p], :] = result[:, :width].astype(tend.dtype)
        for o in range(owners):
            part = pl.ds(p * size + o * capacity, capacity)
            live = place < filled[pl.ds(p * owners + o, 1), :]
            update = result[o * capacity : (o + 1) * capacity, width:]
            old = recalled[part, :].astype(jnp.float32)
            renewed[part, :] = (old + jnp.where(live, update, 0.0)).astype(renewed.dtype)


def network(filled, columns, recalled, w_in, w_mid, w_deep, w_out):
    count, width = columns.shape
    capacity = count // filled.shape[0]
    rows = pl.BlockSpec((ROWS_MLP, width), lambda i: (i, 0))
    counts = pl.BlockSpec((ROWS_MLP // capacity, width), lambda i: (i, 0))
    whole = lambda w: pl.BlockSpec(w.shape, lambda i: (0, 0))
    kernel = lambda *refs: network_kernel(capacity, *refs)
    weights = (w_in, w_mid, w_deep, w_out)
    return pl.pallas_call(
        kernel,
        grid=(count // ROWS_MLP,),
        out_shape=(
            jax.ShapeDtypeStruct((count, width), jnp.bfloat16),
            jax.ShapeDtypeStruct((count, width), jnp.bfloat16),
        ),
        in_specs=[counts, rows, rows] + [whole(w) for w in weights],
        out_specs=(rows, rows),
        scratch_shapes=[pltpu.VMEM(w.shape, w.dtype) for w in weights[:3]],
        compiler_params=pltpu.CompilerParams(vmem_limit_bytes=VMEM_LIMIT),
        cost_estimate=pl.CostEstimate(
            flops=2 * count * sum(w.size for w in weights),
            bytes_accessed=8 * count * width + 2 * sum(w.size for w in weights),
            transcendentals=count * 3 * w_mid.shape[0],
        ),
        name="network",
    )(filled, columns, recalled, *weights)


def finish_kernel(
    ny,
    nx,
    target,
    tend_hbm,
    flow_hbm,
    winds_hbm,
    lat_even,
    lat_odd,
    lon_even,
    lon_odd,
    out_hbm,
    tend,
    flow,
    winds,
    table,
    arrived,
    left_over,
):
    width = flow.shape[0] // (ny * 2)
    lanes = nx // 2
    levels = winds.shape[0] // (4 * ny)
    fields = width // levels
    count = ny * nx
    copies = [
        pltpu.make_async_copy(tend_hbm, tend, arrived.at[0]),
        pltpu.make_async_copy(flow_hbm, flow, arrived.at[1]),
        pltpu.make_async_copy(winds_hbm, winds, arrived.at[2]),
    ]
    for copy in copies:
        copy.start()
    odd = lax.axis_index("span") == 1
    evens, odds = lon_even[...].astype(jnp.float32), lon_odd[...].astype(jnp.float32)
    beside = (jnp.where(odd, evens, odds).T, jnp.where(odd, odds, evens).T)
    odd = lax.axis_index("lat") % 2 == 1
    evens, odds = lat_even[...].astype(jnp.float32), lat_odd[...].astype(jnp.float32)
    south, north = jnp.where(odd, evens, odds), jnp.where(odd, odds, evens)
    lower = table.shape[1]
    uppers = table.shape[0] // width
    shift, mask = log2(lower), lower - 1
    lane = lax.broadcasted_iota(jnp.int32, (width, lanes), 1)
    copies[0].wait()
    for h in range(uppers):
        rows = tend[pl.ds(h * lower, lower), :].astype(jnp.float32)
        table[pl.ds(h * width, width), :] = rows.T.astype(table.dtype)

    def wind(component, y, half):
        first = component * levels * 2 * ny + tile_row(y, half)
        return jnp.concatenate([winds[pl.ds(first, levels, stride=2 * ny), :]] * fields, axis=0)

    for y in range(ny):
        index = jnp.concatenate([target[half, pl.ds(y, 1), :] for half in range(2)], axis=1)
        wanted = jnp.where(index == count, -1, index & mask)
        candidates = jnp.dot(
            table[...], one_hot(wanted, lower), preferred_element_type=jnp.float32
        ).reshape(uppers, width // SUB, SUB, nx)
        upper = jnp.broadcast_to(index >> shift, (SUB, nx))
        change = candidates[0]
        for h in range(1, uppers):
            change = jnp.where((upper == h)[None], candidates[h], change)
        change = change.reshape(width, nx)
        if y == 0:
            copies[1].wait()
            copies[2].wait()
        for half in range(2):
            part = slice(half * lanes, (half + 1) * lanes)
            place = pl.ds(tile_row(y, half), width, stride=2 * ny)
            zonal = wind(0, y, half)
            inflow = -jnp.minimum(zonal, 0.0) if half else jnp.maximum(zonal, 0.0)
            edge = jnp.broadcast_to(beside[half][:, y : y + 1], (width, lanes))
            there = lane == (lanes - 1 if half else 0)
            result = flow[place, :] + jnp.where(there, inflow * edge, 0.0)
            if y == 0:
                result = result + jnp.maximum(wind(1, y, half), 0.0) * south[:, part]
            if y == ny - 1:
                result = result - jnp.minimum(wind(1, y, half), 0.0) * north[:, part]
            flow[place, :] = result + change[:, part]
    pieces = left_over.shape[0]
    size = flow.shape[0] // pieces
    sends = []
    for p in range(pieces):
        rows = pl.ds(p * size, size)
        sends.append(pltpu.make_async_copy(flow.at[rows, :], out_hbm.at[rows, :], left_over.at[p]))
        sends[-1].start()
    for send in sends:
        send.wait()


def finish(target, tend, flow, winds, *edges):
    _, ny, lanes = target.shape
    nx = 2 * lanes
    count, width = tend.shape
    uppers = 8
    vmem = pl.BlockSpec(memory_space=pltpu.VMEM)
    hbm = pl.BlockSpec(memory_space=pl.ANY)
    kernel = lambda *refs: finish_kernel(ny, nx, *refs)
    return pl.pallas_call(
        kernel,
        out_shape=jax.ShapeDtypeStruct(flow.shape, jnp.float32),
        in_specs=[vmem, hbm, hbm, hbm, vmem, vmem, vmem, vmem],
        out_specs=hbm,
        scratch_shapes=[
            pltpu.VMEM(tend.shape, tend.dtype),
            pltpu.VMEM(flow.shape, jnp.float32),
            pltpu.VMEM(winds.shape, jnp.float32),
            pltpu.VMEM((uppers * width, count // uppers), jnp.bfloat16),
            pltpu.SemaphoreType.DMA((3,)),
            pltpu.SemaphoreType.DMA((4,)),
        ],
        compiler_params=pltpu.CompilerParams(vmem_limit_bytes=VMEM_LIMIT),
        cost_estimate=pl.CostEstimate(
            flops=2 * count * count * width,
            bytes_accessed=14 * count * width,
            transcendentals=0,
        ),
        name="finish",
    )(target, tend, flow, winds, *edges)


def to_tiles(field):
    fields, levels, ny, nx = field.shape
    tiles = field.reshape(fields * levels, ny // SUB, SUB, 2, nx // 2)
    return tiles.transpose(0, 1, 3, 2, 4).reshape(fields * levels * ny * 2, nx // 2)


def from_tiles(tiles, shape):
    fields, levels, ny, nx = shape
    field = tiles.reshape(fields * levels, ny // SUB, 2, SUB, nx // 2)
    return field.transpose(0, 1, 3, 2, 4).reshape(shape)


def body(state, winds, memory, w_in, w_mid, w_deep, w_out, dest, slot, convect):
    group = lax.axis_size(GROUP_AXES)

    recalled = exchange(memory)
    flat_state, flat_winds = to_tiles(state), to_tiles(winds)
    columns, lat_even, lat_odd, lon_even, lon_odd, target, filled, flow = dispatch(
        dest, slot, convect, flat_state, flat_winds, group
    )
    loop = ("lon", "span")
    lon_even = swapped(lon_even, loop, 0, True)
    lon_odd = swapped(lon_odd, loop, 1, True)
    lat_even = swapped(lat_even, "lat", 0, False)
    lat_odd = swapped(lat_odd, "lat", 1, False)
    tend, renewed = network(filled, columns, recalled, w_in, w_mid, w_deep, w_out)
    edges = (lat_even, lat_odd, lon_even)
    renewed, edges = lax.optimization_barrier((renewed, edges))
    new_memory = exchange(renewed)
    new_state = finish(target, tend, flow, flat_winds, *edges, lon_odd)
    return from_tiles(new_state, state.shape), new_memory


def solution(mesh):
    field = P(None, None, "lat", ("lon", "span"))
    slots = P(("lon", "lat", "span"), None)
    plane = P("lat", ("lon", "span"))
    in_specs = (field, field, slots, P(), P(), P(), P(), plane, plane, plane)
    return jax.shard_map(
        body, mesh=mesh, in_specs=in_specs, out_specs=(field, slots), check_vma=False
    )
```

```python
import jax
import jax.numpy as jnp
from jax import lax
from jax.experimental import pallas as pl
from jax.experimental.pallas import tpu as pltpu
from jax.sharding import PartitionSpec as P

GROUP_AXES = ("lat", "span")
MIB = 1024 * 1024
ROWS_MLP = 2048
PART = 1024
VMEM_LIMIT = 60 * MIB
SUB = 8


def swapped(edge, axis, first, wrap):
    count = lax.axis_size(axis)
    pairs = [(i, (i + 1) % count) for i in range(first, count if wrap else count - 1, 2)]
    return lax.ppermute(edge, axis, pairs + [(j, i) for i, j in pairs])


def exchange(rows):
    return lax.all_to_all(rows, GROUP_AXES, split_axis=0, concat_axis=0, tiled=True)


def tile_row(y, half):
    return (y // SUB) * (2 * SUB) + half * SUB + y % SUB


def one_hot(index, size):
    lanes = index.shape[1]
    step = 2 * SUB
    index = jnp.broadcast_to(index, (step, lanes)).astype(jnp.int16)
    place = lax.broadcasted_iota(jnp.int32, (step, lanes), 0).astype(jnp.int16)
    one, zero = jnp.ones((step, lanes), jnp.bfloat16), jnp.zeros((step, lanes), jnp.bfloat16)
    blocks = [
        jnp.where(index == place + jnp.int16(start), one, zero) for start in range(0, size, step)
    ]
    return jnp.concatenate(blocks, axis=0)


def log2(size):
    return size.bit_length() - 1


def dispatch_kernel(
    ny,
    nx,
    dest,
    slot,
    convect,
    state_hbm,
    slots,
    lat_even,
    lat_odd,
    lon_even,
    lon_odd,
    target,
    filled,
    state,
    chosen,
    choice,
    total,
    edges,
    arrived,
):
    load = pltpu.make_async_copy(state_hbm, state, arrived)
    load.start()
    width = state.shape[0] // (ny * 2)
    lanes = nx // 2
    lower = choice.shape[1]
    uppers = chosen.shape[2] // width
    depth = choice.shape[2]
    lines = depth // nx
    steps = ny // lines
    group = filled.shape[0]
    capacity = ny * nx // group
    shift, mask = log2(lower), lower - 1
    live = convect[...] > 0
    goal = jnp.where(live, dest[...] * capacity + slot[...], ny * nx)
    owner = goal >> log2(capacity)
    owners = lax.broadcasted_iota(jnp.int32, (group, nx), 0)
    counts = jnp.zeros((group, nx), jnp.int32)
    for y in range(ny):
        counts += (owners == owner[y : y + 1]).astype(jnp.int32)
    filled[...] = jnp.broadcast_to(jnp.sum(counts, axis=1, keepdims=True), filled.shape)
    for half in range(2):
        target[half] = goal[:, half * lanes : (half + 1) * lanes]
    goals = goal.T
    load.wait()

    def build(g, b):
        for line in range(lines):
            y = g * lines + line
            choice[b, :, pl.ds(line * nx, nx)] = one_hot(goal[y : y + 1] & mask, lower)
            upper = jnp.broadcast_to(goals[:, y : y + 1] >> shift, (nx, width)).astype(jnp.int16)
            for half in range(2):
                part = slice(half * lanes, (half + 1) * lanes)
                values = state[pl.ds(tile_row(y, half), width, stride=2 * ny), :].T
                if half == 0:
                    edges[pl.ds(y, 1), :] = values[:1]
                else:
                    edges[pl.ds(ny + y, 1), :] = values[lanes - 1 :]
                values = values.astype(jnp.bfloat16)
                rows = pl.ds(line * nx + half * lanes, lanes)
                for h in range(uppers):
                    chosen[b, rows, pl.ds(h * width, width)] = jnp.where(
                        upper[part] == h, values, jnp.zeros_like(values)
                    )

    def multiply(g, b):
        product = jnp.dot(choice[b], chosen[b], preferred_element_type=jnp.float32)
        if g == 0:
            total[...] = product
        else:
            total[...] += product

    build(0, 0)
    for g in range(steps):
        if g < steps - 1:
            build(g + 1, (g + 1) % 2)
        multiply(g, g % 2)
    for h in range(uppers):
        slots[pl.ds(h * lower, lower), :] = total[:, pl.ds(h * width, width)].astype(slots.dtype)

    odd = lax.axis_index("lat") % 2 == 1
    for half in range(2):
        part = pl.ds(half * lanes, lanes)
        south = state[pl.ds(tile_row(0, half), width, stride=2 * ny), :]
        north = state[pl.ds(tile_row(ny - 1, half), width, stride=2 * ny), :]
        lat_even[:, part] = jnp.where(odd, south, north).astype(lat_even.dtype)
        lat_odd[:, part] = jnp.where(odd, north, south).astype(lat_odd.dtype)
    odd = lax.axis_index("span") == 1
    west, east = edges[pl.ds(0, ny), :], edges[pl.ds(ny, ny), :]
    lon_even[...] = jnp.where(odd, west, east).astype(lon_even.dtype)
    lon_odd[...] = jnp.where(odd, east, west).astype(lon_odd.dtype)


def dispatch(dest, slot, convect, state, group):
    ny, nx = dest.shape
    width, count = state.shape[0] // (ny * 2), ny * nx
    uppers, depth = 4, 4 * nx
    lower = count // uppers
    vmem = pl.BlockSpec(memory_space=pltpu.VMEM)
    kernel = lambda *refs: dispatch_kernel(ny, nx, *refs)
    shape = jax.ShapeDtypeStruct
    return pl.pallas_call(
        kernel,
        out_shape=(
            shape((count, width), jnp.bfloat16),
            shape((width, nx), jnp.bfloat16),
            shape((width, nx), jnp.bfloat16),
            shape((ny, width), jnp.bfloat16),
            shape((ny, width), jnp.bfloat16),
            shape((2, ny, nx // 2), jnp.int32),
            shape((group, width), jnp.int32),
        ),
        in_specs=[vmem, vmem, vmem, pl.BlockSpec(memory_space=pl.ANY)],
        out_specs=(vmem,) * 7,
        scratch_shapes=[
            pltpu.VMEM(state.shape, jnp.float32),
            pltpu.VMEM((2, depth, uppers * width), jnp.bfloat16),
            pltpu.VMEM((2, lower, depth), jnp.bfloat16),
            pltpu.VMEM((lower, uppers * width), jnp.float32),
            pltpu.VMEM((2 * ny, width), jnp.float32),
            pltpu.SemaphoreType.DMA,
        ],
        compiler_params=pltpu.CompilerParams(vmem_limit_bytes=63 * MIB),
        cost_estimate=pl.CostEstimate(
            flops=2 * count * count * width,
            bytes_accessed=6 * count * width,
            transcendentals=0,
        ),
        name="dispatch",
    )(dest, slot, convect, state)


def silu_of_half(half):
    return half + half * jnp.tanh(half)


def network_kernel(
    capacity,
    filled,
    columns,
    recalled,
    w_in,
    w_mid,
    w_deep,
    w_out,
    tend,
    renewed,
    half_in,
    half_mid,
    half_deep,
):
    @pl.when(pl.program_id(0) == 0)
    def _():
        for half, weights in ((half_in, w_in), (half_mid, w_mid), (half_deep, w_deep)):
            half[...] = weights[...] * jnp.bfloat16(0.5)

    width = columns.shape[1]
    size, wide = PART, w_in.shape[1]
    parts = columns.shape[0] // size
    rows = [pl.ds(p * size, size) for p in range(parts)]
    values = [[columns[r, :], recalled[r, :]] for r in rows]
    waiting = []

    def settle():
        sums, kept = waiting.pop(0)
        kept.append(silu_of_half(sums).astype(jnp.bfloat16))

    for weights in (half_in, half_mid, half_deep):
        following = [[] for _ in rows]
        for p in range(parts):
            joined = jnp.concatenate(values[p], axis=1)
            for n in range(weights.shape[1] // wide):
                piece = weights[:, pl.ds(n * wide, wide)]
                sums = jnp.dot(joined, piece, preferred_element_type=jnp.float32)
                waiting.append((sums, following[p]))
                if len(waiting) > 1:
                    settle()
        values = following
    settle()
    owners = size // capacity
    place = lax.broadcasted_iota(jnp.int32, (capacity, width), 0)
    for p in range(parts):
        joined = jnp.concatenate(values[p], axis=1)
        result = jnp.dot(joined, w_out[...], preferred_element_type=jnp.float32)
        tend[rows[p], :] = result[:, :width].astype(tend.dtype)
        for o in range(owners):
            part = pl.ds(p * size + o * capacity, capacity)
            live = place < filled[pl.ds(p * owners + o, 1), :]
            update = result[o * capacity : (o + 1) * capacity, width:]
            old = recalled[part, :].astype(jnp.float32)
            renewed[part, :] = (old + jnp.where(live, update, 0.0)).astype(renewed.dtype)


def network(filled, columns, recalled, w_in, w_mid, w_deep, w_out):
    count, width = columns.shape
    capacity = count // filled.shape[0]
    rows = pl.BlockSpec((ROWS_MLP, width), lambda i: (i, 0))
    counts = pl.BlockSpec((ROWS_MLP // capacity, width), lambda i: (i, 0))
    whole = lambda w: pl.BlockSpec(w.shape, lambda i: (0, 0))
    kernel = lambda *refs: network_kernel(capacity, *refs)
    weights = (w_in, w_mid, w_deep, w_out)
    return pl.pallas_call(
        kernel,
        grid=(count // ROWS_MLP,),
        out_shape=(
            jax.ShapeDtypeStruct((count, width), jnp.bfloat16),
            jax.ShapeDtypeStruct((count, width), jnp.bfloat16),
        ),
        in_specs=[counts, rows, rows] + [whole(w) for w in weights],
        out_specs=(rows, rows),
        scratch_shapes=[pltpu.VMEM(w.shape, w.dtype) for w in weights[:3]],
        compiler_params=pltpu.CompilerParams(vmem_limit_bytes=VMEM_LIMIT),
        cost_estimate=pl.CostEstimate(
            flops=2 * count * sum(w.size for w in weights),
            bytes_accessed=8 * count * width + 2 * sum(w.size for w in weights),
            transcendentals=count * 3 * w_mid.shape[0],
        ),
        name="network",
    )(filled, columns, recalled, *weights)


def finish_kernel(
    ny,
    nx,
    target,
    tend_hbm,
    state_hbm,
    winds_hbm,
    lat_even,
    lat_odd,
    lon_even,
    lon_odd,
    out_hbm,
    tend,
    state,
    winds,
    table,
    low,
    high,
    moved,
    flow,
    arrived,
    left_over,
):
    width = state.shape[0] // (ny * 2)
    lanes = nx // 2
    subs = ny // SUB
    levels = winds.shape[0] // (4 * ny)
    count = ny * nx
    pitch = moved.shape[0] // width
    copies = [
        pltpu.make_async_copy(tend_hbm, tend, arrived.at[0]),
        pltpu.make_async_copy(state_hbm, state, arrived.at[1]),
        pltpu.make_async_copy(winds_hbm, winds, arrived.at[2]),
    ]
    for copy in copies:
        copy.start()
    odd = lax.axis_index("span") == 1
    evens, odds = lon_even[...].astype(jnp.float32), lon_odd[...].astype(jnp.float32)
    west = jnp.where(odd, evens, odds)
    east = jnp.where(odd, odds, evens)
    odd = lax.axis_index("lat") % 2 == 1
    for half in range(2):
        part = pl.ds(half * lanes, lanes)
        evens, odds = lat_even[:, part].astype(jnp.float32), lat_odd[:, part].astype(jnp.float32)
        low[half] = jnp.where(odd, evens, odds)
        high[half] = jnp.where(odd, odds, evens)
    lower = table.shape[1]
    uppers = table.shape[0] // width
    shift, mask = log2(lower), lower - 1
    copies[0].wait()
    for h in range(uppers):
        rows = tend[pl.ds(h * lower, lower), :].astype(jnp.float32)
        table[pl.ds(h * width, width), :] = rows.T.astype(table.dtype)

    lane = lax.broadcasted_iota(jnp.int32, (SUB, lanes), 1)
    line = lax.broadcasted_iota(jnp.int32, (SUB, lanes), 0)
    tiles = [(sub, half) for sub in range(subs) for half in range(2)]

    def block(r, sub, half):
        return pl.ds(r * (2 * ny) + (sub * 2 + half) * SUB, SUB)

    def move(y):
        index = jnp.concatenate([target[half, pl.ds(y, 1), :] for half in range(2)], axis=1)
        wanted = jnp.where(index == count, -1, index & mask)
        candidates = jnp.dot(
            table[...], one_hot(wanted, lower), preferred_element_type=jnp.float32
        ).reshape(uppers, width // SUB, SUB, nx)
        upper = jnp.broadcast_to(index >> shift, (SUB, nx))
        change = candidates[0]
        for h in range(1, uppers):
            change = jnp.where((upper == h)[None], candidates[h], change)
        change = change.reshape(width, nx)
        for half in range(2):
            place = pl.ds(tile_row(y, half), width, stride=pitch)
            moved[place, :] = change[:, half * lanes : (half + 1) * lanes]

    def advect(k):
        zonal = {t: winds[block(k, *t), :] for t in tiles}
        meridional = {t: winds[block(levels + k, *t), :] for t in tiles}
        for f in range(width // levels):
            r = f * levels + k
            s = {t: state[block(r, *t), :] for t in tiles}
            first = pltpu.roll(west, (width - r) % width, axis=1)
            last = pltpu.roll(east, width - 1 - r, axis=1)
            up = {t: pltpu.roll(s[t], 1, axis=1) for t in tiles}
            down = {t: pltpu.roll(s[t], lanes - 1, axis=1) for t in tiles}
            rise = {t: pltpu.roll(s[t], 1, axis=0) for t in tiles}
            fall = {t: pltpu.roll(s[t], SUB - 1, axis=0) for t in tiles}
            for sub, half in tiles:
                t = (sub, half)
                edge = slice(sub * SUB, (sub + 1) * SUB)
                left = jnp.where(lane == 0, up[sub, 0] if half else first[edge], up[t])
                right = jnp.where(lane == lanes - 1, last[edge] if half else down[sub, 1], down[t])
                under = rise[sub - 1, half] if sub else low[half, pl.ds(r, 1), :]
                over = fall[sub + 1, half] if sub < subs - 1 else high[half, pl.ds(r, 1), :]
                below = jnp.where(line == 0, under, rise[t])
                above = jnp.where(line == SUB - 1, over, fall[t])
                flow[block(r, *t), :] = (
                    s[t]
                    - jnp.maximum(zonal[t], 0.0) * (s[t] - left)
                    - jnp.minimum(zonal[t], 0.0) * (right - s[t])
                    - jnp.maximum(meridional[t], 0.0) * (s[t] - below)
                    - jnp.minimum(meridional[t], 0.0) * (above - s[t])
                )

    ahead = 2
    share = levels // (ny - ahead) + 1
    for y in range(ny):
        move(y)
        if y == ahead - 1:
            copies[1].wait()
            copies[2].wait()
        start = (y - ahead) * share
        for k in range(max(start, 0), max(min(start + share, levels), 0)):
            advect(k)
    pieces = left_over.shape[0]
    size = state.shape[0] // pieces
    sends = []
    for p in range(pieces):
        rows = pl.ds(p * size, size)
        for r in range(p * width // pieces, (p + 1) * width // pieces):
            here = pl.ds(r * 2 * ny, 2 * ny)
            flow[here, :] = flow[here, :] + moved[pl.ds(r * pitch, 2 * ny), :]
        sends.append(pltpu.make_async_copy(flow.at[rows, :], out_hbm.at[rows, :], left_over.at[p]))
        sends[-1].start()
    for send in sends:
        send.wait()


def finish(target, tend, state, winds, *edges):
    _, ny, lanes = target.shape
    nx = 2 * lanes
    count, width = tend.shape
    uppers = 8
    vmem = pl.BlockSpec(memory_space=pltpu.VMEM)
    hbm = pl.BlockSpec(memory_space=pl.ANY)
    kernel = lambda *refs: finish_kernel(ny, nx, *refs)
    return pl.pallas_call(
        kernel,
        out_shape=jax.ShapeDtypeStruct(state.shape, jnp.float32),
        in_specs=[vmem, hbm, hbm, hbm, vmem, vmem, vmem, vmem],
        out_specs=hbm,
        scratch_shapes=[
            pltpu.VMEM(tend.shape, tend.dtype),
            pltpu.VMEM(state.shape, jnp.float32),
            pltpu.VMEM(winds.shape, jnp.float32),
            pltpu.VMEM((uppers * width, count // uppers), jnp.bfloat16),
            pltpu.VMEM((2, width, lanes), jnp.float32),
            pltpu.VMEM((2, width, lanes), jnp.float32),
            pltpu.VMEM((width * (2 * ny + SUB), lanes), jnp.float32),
            pltpu.VMEM(state.shape, jnp.float32),
            pltpu.SemaphoreType.DMA((3,)),
            pltpu.SemaphoreType.DMA((4,)),
        ],
        compiler_params=pltpu.CompilerParams(vmem_limit_bytes=56 * MIB),
        cost_estimate=pl.CostEstimate(
            flops=2 * count * count * width,
            bytes_accessed=14 * count * width,
            transcendentals=0,
        ),
        name="finish",
    )(target, tend, state, winds, *edges)


def to_tiles(field):
    fields, levels, ny, nx = field.shape
    tiles = field.reshape(fields * levels, ny // SUB, SUB, 2, nx // 2)
    return tiles.transpose(0, 1, 3, 2, 4).reshape(fields * levels * ny * 2, nx // 2)


def from_tiles(tiles, shape):
    fields, levels, ny, nx = shape
    field = tiles.reshape(fields * levels, ny // SUB, 2, SUB, nx // 2)
    return field.transpose(0, 1, 3, 2, 4).reshape(shape)


def body(state, winds, memory, w_in, w_mid, w_deep, w_out, dest, slot, convect):
    group = lax.axis_size(GROUP_AXES)

    recalled = exchange(memory)
    flat_state, flat_winds = to_tiles(state), to_tiles(winds)
    columns, lat_even, lat_odd, lon_even, lon_odd, target, filled = dispatch(
        dest, slot, convect, flat_state, group
    )
    loop = ("lon", "span")
    lon_even = swapped(lon_even, loop, 0, True)
    lon_odd = swapped(lon_odd, loop, 1, True)
    lat_even = swapped(lat_even, "lat", 0, False)
    lat_odd = swapped(lat_odd, "lat", 1, False)
    tend, renewed = network(filled, columns, recalled, w_in, w_mid, w_deep, w_out)
    edges = (lat_even, lat_odd, lon_even)
    renewed, edges = lax.optimization_barrier((renewed, edges))
    new_memory = exchange(renewed)
    new_state = finish(target, tend, flat_state, flat_winds, *edges, lon_odd)
    return from_tiles(new_state, state.shape), new_memory


def solution(mesh):
    field = P(None, None, "lat", ("lon", "span"))
    slots = P(("lon", "lat", "span"), None)
    plane = P("lat", ("lon", "span"))
    in_specs = (field, field, slots, P(), P(), P(), P(), plane, plane, plane)
    return jax.shard_map(
        body, mesh=mesh, in_specs=in_specs, out_specs=(field, slots), check_vma=False
    )
```

```python
import jax
import jax.numpy as jnp
from jax import lax
from jax.experimental import pallas as pl
from jax.experimental.pallas import tpu as pltpu
from jax.sharding import PartitionSpec as P

GROUP_AXES = ("lat", "span")
MIB = 1024 * 1024
ROWS_MLP = 2048
PART = 512
VMEM_LIMIT = 60 * MIB
SUB = 8


def swapped(edge, axis, first, wrap):
    count = lax.axis_size(axis)
    pairs = [(i, (i + 1) % count) for i in range(first, count if wrap else count - 1, 2)]
    return lax.ppermute(edge, axis, pairs + [(j, i) for i, j in pairs])


def exchange(rows):
    return lax.all_to_all(rows, GROUP_AXES, split_axis=0, concat_axis=0, tiled=True)


def tile_row(y, half):
    return (y // SUB) * (2 * SUB) + half * SUB + y % SUB


def one_hot(index, size):
    lanes = index.shape[1]
    step = 2 * SUB
    index = jnp.broadcast_to(index, (step, lanes)).astype(jnp.int16)
    place = lax.broadcasted_iota(jnp.int32, (step, lanes), 0).astype(jnp.int16)
    one, zero = jnp.ones((step, lanes), jnp.bfloat16), jnp.zeros((step, lanes), jnp.bfloat16)
    blocks = [
        jnp.where(index == place + jnp.int16(start), one, zero) for start in range(0, size, step)
    ]
    return jnp.concatenate(blocks, axis=0)


def log2(size):
    return size.bit_length() - 1


def dispatch_kernel(
    ny,
    nx,
    dest,
    slot,
    convect,
    state_hbm,
    slots,
    lat_even,
    lat_odd,
    lon_even,
    lon_odd,
    target,
    filled,
    state,
    chosen,
    choice,
    total,
    edges,
    arrived,
):
    load = pltpu.make_async_copy(state_hbm, state, arrived)
    load.start()
    width = state.shape[0] // (ny * 2)
    lanes = nx // 2
    lower = choice.shape[1]
    uppers = chosen.shape[2] // width
    depth = choice.shape[2]
    lines = depth // nx
    steps = ny // lines
    group = filled.shape[0]
    capacity = ny * nx // group
    shift, mask = log2(lower), lower - 1
    live = convect[...] > 0
    goal = jnp.where(live, dest[...] * capacity + slot[...], ny * nx)
    owner = goal >> log2(capacity)
    owners = lax.broadcasted_iota(jnp.int32, (group, nx), 0)
    counts = jnp.zeros((group, nx), jnp.int32)
    for y in range(ny):
        counts += (owners == owner[y : y + 1]).astype(jnp.int32)
    filled[...] = jnp.broadcast_to(jnp.sum(counts, axis=1, keepdims=True), filled.shape)
    for half in range(2):
        target[half] = goal[:, half * lanes : (half + 1) * lanes]
    goals = goal.T
    load.wait()

    def build(g, b):
        for line in range(lines):
            y = g * lines + line
            choice[b, :, pl.ds(line * nx, nx)] = one_hot(goal[y : y + 1] & mask, lower)
            upper = jnp.broadcast_to(goals[:, y : y + 1] >> shift, (nx, width)).astype(jnp.int16)
            for half in range(2):
                part = slice(half * lanes, (half + 1) * lanes)
                values = state[pl.ds(tile_row(y, half), width, stride=2 * ny), :].T
                if half == 0:
                    edges[pl.ds(y, 1), :] = values[:1]
                else:
                    edges[pl.ds(ny + y, 1), :] = values[lanes - 1 :]
                values = values.astype(jnp.bfloat16)
                rows = pl.ds(line * nx + half * lanes, lanes)
                for h in range(uppers):
                    chosen[b, rows, pl.ds(h * width, width)] = jnp.where(
                        upper[part] == h, values, jnp.zeros_like(values)
                    )

    def multiply(g, b):
        product = jnp.dot(choice[b], chosen[b], preferred_element_type=jnp.float32)
        if g == 0:
            total[...] = product
        else:
            total[...] += product

    build(0, 0)
    for g in range(steps):
        if g < steps - 1:
            build(g + 1, (g + 1) % 2)
        multiply(g, g % 2)
    for h in range(uppers):
        slots[pl.ds(h * lower, lower), :] = total[:, pl.ds(h * width, width)].astype(slots.dtype)

    odd = lax.axis_index("lat") % 2 == 1
    for half in range(2):
        part = pl.ds(half * lanes, lanes)
        south = state[pl.ds(tile_row(0, half), width, stride=2 * ny), :]
        north = state[pl.ds(tile_row(ny - 1, half), width, stride=2 * ny), :]
        lat_even[:, part] = jnp.where(odd, south, north).astype(lat_even.dtype)
        lat_odd[:, part] = jnp.where(odd, north, south).astype(lat_odd.dtype)
    odd = lax.axis_index("span") == 1
    west, east = edges[pl.ds(0, ny), :], edges[pl.ds(ny, ny), :]
    lon_even[...] = jnp.where(odd, west, east).astype(lon_even.dtype)
    lon_odd[...] = jnp.where(odd, east, west).astype(lon_odd.dtype)


def dispatch(dest, slot, convect, state, group):
    ny, nx = dest.shape
    width, count = state.shape[0] // (ny * 2), ny * nx
    uppers, depth = 4, 4 * nx
    lower = count // uppers
    vmem = pl.BlockSpec(memory_space=pltpu.VMEM)
    kernel = lambda *refs: dispatch_kernel(ny, nx, *refs)
    shape = jax.ShapeDtypeStruct
    return pl.pallas_call(
        kernel,
        out_shape=(
            shape((count, width), jnp.bfloat16),
            shape((width, nx), jnp.bfloat16),
            shape((width, nx), jnp.bfloat16),
            shape((ny, width), jnp.bfloat16),
            shape((ny, width), jnp.bfloat16),
            shape((2, ny, nx // 2), jnp.int32),
            shape((group, width), jnp.int32),
        ),
        in_specs=[vmem, vmem, vmem, pl.BlockSpec(memory_space=pl.ANY)],
        out_specs=(vmem,) * 7,
        scratch_shapes=[
            pltpu.VMEM(state.shape, jnp.float32),
            pltpu.VMEM((2, depth, uppers * width), jnp.bfloat16),
            pltpu.VMEM((2, lower, depth), jnp.bfloat16),
            pltpu.VMEM((lower, uppers * width), jnp.float32),
            pltpu.VMEM((2 * ny, width), jnp.float32),
            pltpu.SemaphoreType.DMA,
        ],
        compiler_params=pltpu.CompilerParams(vmem_limit_bytes=63 * MIB),
        cost_estimate=pl.CostEstimate(
            flops=2 * count * count * width,
            bytes_accessed=6 * count * width,
            transcendentals=0,
        ),
        name="dispatch",
    )(dest, slot, convect, state)


def silu_of_half(half):
    return half + half * jnp.tanh(half)


def network_kernel(
    capacity,
    filled,
    columns,
    recalled,
    w_in,
    w_mid,
    w_deep,
    w_out,
    tend,
    renewed,
    half_in,
    half_mid,
    half_deep,
):
    @pl.when(pl.program_id(0) == 0)
    def _():
        for half, weights in ((half_in, w_in), (half_mid, w_mid), (half_deep, w_deep)):
            half[...] = weights[...] * jnp.bfloat16(0.5)

    width = columns.shape[1]
    size, wide = PART, w_in.shape[1]
    parts = columns.shape[0] // size
    rows = [pl.ds(p * size, size) for p in range(parts)]
    values = [[columns[r, :], recalled[r, :]] for r in rows]
    waiting = []

    def settle():
        sums, kept = waiting.pop(0)
        kept.append(silu_of_half(sums).astype(jnp.bfloat16))

    for weights in (half_in, half_mid, half_deep):
        following = [[] for _ in rows]
        for p in range(parts):
            joined = jnp.concatenate(values[p], axis=1)
            for n in range(weights.shape[1] // wide):
                piece = weights[:, pl.ds(n * wide, wide)]
                sums = jnp.dot(joined, piece, preferred_element_type=jnp.float32)
                waiting.append((sums, following[p]))
                if len(waiting) > 1:
                    settle()
        values = following
    settle()
    owners = size // capacity
    place = lax.broadcasted_iota(jnp.int32, (capacity, width), 0)
    for p in range(parts):
        joined = jnp.concatenate(values[p], axis=1)
        result = jnp.dot(joined, w_out[...], preferred_element_type=jnp.float32)
        tend[rows[p], :] = result[:, :width].astype(tend.dtype)
        for o in range(owners):
            part = pl.ds(p * size + o * capacity, capacity)
            live = place < filled[pl.ds(p * owners + o, 1), :]
            update = result[o * capacity : (o + 1) * capacity, width:]
            old = recalled[part, :].astype(jnp.float32)
            renewed[part, :] = (old + jnp.where(live, update, 0.0)).astype(renewed.dtype)


def network(filled, columns, recalled, w_in, w_mid, w_deep, w_out):
    count, width = columns.shape
    capacity = count // filled.shape[0]
    rows = pl.BlockSpec((ROWS_MLP, width), lambda i: (i, 0))
    counts = pl.BlockSpec((ROWS_MLP // capacity, width), lambda i: (i, 0))
    whole = lambda w: pl.BlockSpec(w.shape, lambda i: (0, 0))
    kernel = lambda *refs: network_kernel(capacity, *refs)
    weights = (w_in, w_mid, w_deep, w_out)
    return pl.pallas_call(
        kernel,
        grid=(count // ROWS_MLP,),
        out_shape=(
            jax.ShapeDtypeStruct((count, width), jnp.bfloat16),
            jax.ShapeDtypeStruct((count, width), jnp.bfloat16),
        ),
        in_specs=[counts, rows, rows] + [whole(w) for w in weights],
        out_specs=(rows, rows),
        scratch_shapes=[pltpu.VMEM(w.shape, w.dtype) for w in weights[:3]],
        compiler_params=pltpu.CompilerParams(vmem_limit_bytes=VMEM_LIMIT),
        cost_estimate=pl.CostEstimate(
            flops=2 * count * sum(w.size for w in weights),
            bytes_accessed=8 * count * width + 2 * sum(w.size for w in weights),
            transcendentals=count * 3 * w_mid.shape[0],
        ),
        name="network",
    )(filled, columns, recalled, *weights)


def finish_kernel(
    ny,
    nx,
    target,
    tend_hbm,
    state_hbm,
    winds_hbm,
    lat_even,
    lat_odd,
    lon_even,
    lon_odd,
    out_hbm,
    tend,
    state,
    winds,
    table,
    low,
    high,
    moved,
    flow,
    arrived,
    left_over,
):
    width = state.shape[0] // (ny * 2)
    lanes = nx // 2
    subs = ny // SUB
    levels = winds.shape[0] // (4 * ny)
    count = ny * nx
    pitch = moved.shape[0] // width
    copies = [
        pltpu.make_async_copy(tend_hbm, tend, arrived.at[0]),
        pltpu.make_async_copy(state_hbm, state, arrived.at[1]),
        pltpu.make_async_copy(winds_hbm, winds, arrived.at[2]),
    ]
    for copy in copies:
        copy.start()
    odd = lax.axis_index("span") == 1
    evens, odds = lon_even[...].astype(jnp.float32), lon_odd[...].astype(jnp.float32)
    west = jnp.where(odd, evens, odds)
    east = jnp.where(odd, odds, evens)
    odd = lax.axis_index("lat") % 2 == 1
    for half in range(2):
        part = pl.ds(half * lanes, lanes)
        evens, odds = lat_even[:, part].astype(jnp.float32), lat_odd[:, part].astype(jnp.float32)
        low[half] = jnp.where(odd, evens, odds)
        high[half] = jnp.where(odd, odds, evens)
    lower = table.shape[1]
    uppers = table.shape[0] // width
    shift, mask = log2(lower), lower - 1
    copies[0].wait()
    for h in range(uppers):
        rows = tend[pl.ds(h * lower, lower), :].astype(jnp.float32)
        table[pl.ds(h * width, width), :] = rows.T.astype(table.dtype)

    lane = lax.broadcasted_iota(jnp.int32, (SUB, lanes), 1)
    line = lax.broadcasted_iota(jnp.int32, (SUB, lanes), 0)
    tiles = [(sub, half) for sub in range(subs) for half in range(2)]

    def block(r, sub, half):
        return pl.ds(r * (2 * ny) + (sub * 2 + half) * SUB, SUB)

    def move(y):
        index = jnp.concatenate([target[half, pl.ds(y, 1), :] for half in range(2)], axis=1)
        wanted = jnp.where(index == count, -1, index & mask)
        candidates = jnp.dot(
            table[...], one_hot(wanted, lower), preferred_element_type=jnp.float32
        ).reshape(uppers, width // SUB, SUB, nx)
        upper = jnp.broadcast_to(index >> shift, (SUB, nx))
        change = candidates[0]
        for h in range(1, uppers):
            change = jnp.where((upper == h)[None], candidates[h], change)
        change = change.reshape(width, nx)
        for half in range(2):
            place = pl.ds(tile_row(y, half), width, stride=pitch)
            moved[place, :] = change[:, half * lanes : (half + 1) * lanes]

    def advect(k):
        zonal = {t: winds[block(k, *t), :] for t in tiles}
        meridional = {t: winds[block(levels + k, *t), :] for t in tiles}
        for f in range(width // levels):
            r = f * levels + k
            s = {t: state[block(r, *t), :] for t in tiles}
            first = pltpu.roll(west, (width - r) % width, axis=1)
            last = pltpu.roll(east, width - 1 - r, axis=1)
            up = {t: pltpu.roll(s[t], 1, axis=1) for t in tiles}
            down = {t: pltpu.roll(s[t], lanes - 1, axis=1) for t in tiles}
            rise = {t: pltpu.roll(s[t], 1, axis=0) for t in tiles}
            fall = {t: pltpu.roll(s[t], SUB - 1, axis=0) for t in tiles}
            for sub, half in tiles:
                t = (sub, half)
                edge = slice(sub * SUB, (sub + 1) * SUB)
                left = jnp.where(lane == 0, up[sub, 0] if half else first[edge], up[t])
                right = jnp.where(lane == lanes - 1, last[edge] if half else down[sub, 1], down[t])
                under = rise[sub - 1, half] if sub else low[half, pl.ds(r, 1), :]
                over = fall[sub + 1, half] if sub < subs - 1 else high[half, pl.ds(r, 1), :]
                below = jnp.where(line == 0, under, rise[t])
                above = jnp.where(line == SUB - 1, over, fall[t])
                flow[block(r, *t), :] = (
                    s[t]
                    - jnp.maximum(zonal[t], 0.0) * (s[t] - left)
                    - jnp.minimum(zonal[t], 0.0) * (right - s[t])
                    - jnp.maximum(meridional[t], 0.0) * (s[t] - below)
                    - jnp.minimum(meridional[t], 0.0) * (above - s[t])
                )

    ahead = 2
    share = levels // (ny - ahead) + 1
    for y in range(ny):
        move(y)
        if y == ahead - 1:
            copies[1].wait()
            copies[2].wait()
        start = (y - ahead) * share
        for k in range(max(start, 0), max(min(start + share, levels), 0)):
            advect(k)
    pieces = left_over.shape[0]
    size = state.shape[0] // pieces
    sends = []
    for p in range(pieces):
        rows = pl.ds(p * size, size)
        for r in range(p * width // pieces, (p + 1) * width // pieces):
            here = pl.ds(r * 2 * ny, 2 * ny)
            flow[here, :] = flow[here, :] + moved[pl.ds(r * pitch, 2 * ny), :]
        sends.append(pltpu.make_async_copy(flow.at[rows, :], out_hbm.at[rows, :], left_over.at[p]))
        sends[-1].start()
    for send in sends:
        send.wait()


def finish(target, tend, state, winds, *edges):
    _, ny, lanes = target.shape
    nx = 2 * lanes
    count, width = tend.shape
    uppers = 8
    vmem = pl.BlockSpec(memory_space=pltpu.VMEM)
    hbm = pl.BlockSpec(memory_space=pl.ANY)
    kernel = lambda *refs: finish_kernel(ny, nx, *refs)
    return pl.pallas_call(
        kernel,
        out_shape=jax.ShapeDtypeStruct(state.shape, jnp.float32),
        in_specs=[vmem, hbm, hbm, hbm, vmem, vmem, vmem, vmem],
        out_specs=hbm,
        scratch_shapes=[
            pltpu.VMEM(tend.shape, tend.dtype),
            pltpu.VMEM(state.shape, jnp.float32),
            pltpu.VMEM(winds.shape, jnp.float32),
            pltpu.VMEM((uppers * width, count // uppers), jnp.bfloat16),
            pltpu.VMEM((2, width, lanes), jnp.float32),
            pltpu.VMEM((2, width, lanes), jnp.float32),
            pltpu.VMEM((width * (2 * ny + SUB), lanes), jnp.float32),
            pltpu.VMEM(state.shape, jnp.float32),
            pltpu.SemaphoreType.DMA((3,)),
            pltpu.SemaphoreType.DMA((4,)),
        ],
        compiler_params=pltpu.CompilerParams(vmem_limit_bytes=56 * MIB),
        cost_estimate=pl.CostEstimate(
            flops=2 * count * count * width,
            bytes_accessed=14 * count * width,
            transcendentals=0,
        ),
        name="finish",
    )(target, tend, state, winds, *edges)


def to_tiles(field):
    fields, levels, ny, nx = field.shape
    tiles = field.reshape(fields * levels, ny // SUB, SUB, 2, nx // 2)
    return tiles.transpose(0, 1, 3, 2, 4).reshape(fields * levels * ny * 2, nx // 2)


def from_tiles(tiles, shape):
    fields, levels, ny, nx = shape
    field = tiles.reshape(fields * levels, ny // SUB, 2, SUB, nx // 2)
    return field.transpose(0, 1, 3, 2, 4).reshape(shape)


def body(state, winds, memory, w_in, w_mid, w_deep, w_out, dest, slot, convect):
    group = lax.axis_size(GROUP_AXES)

    recalled = exchange(memory)
    flat_state, flat_winds = to_tiles(state), to_tiles(winds)
    columns, lat_even, lat_odd, lon_even, lon_odd, target, filled = dispatch(
        dest, slot, convect, flat_state, group
    )
    loop = ("lon", "span")
    lon_even = swapped(lon_even, loop, 0, True)
    lon_odd = swapped(lon_odd, loop, 1, True)
    lat_even = swapped(lat_even, "lat", 0, False)
    lat_odd = swapped(lat_odd, "lat", 1, False)
    tend, renewed = network(filled, columns, recalled, w_in, w_mid, w_deep, w_out)
    edges = (lat_even, lat_odd, lon_even)
    renewed, edges = lax.optimization_barrier((renewed, edges))
    new_memory = exchange(renewed)
    new_state = finish(target, tend, flat_state, flat_winds, *edges, lon_odd)
    return from_tiles(new_state, state.shape), new_memory


def solution(mesh):
    field = P(None, None, "lat", ("lon", "span"))
    slots = P(("lon", "lat", "span"), None)
    plane = P("lat", ("lon", "span"))
    in_specs = (field, field, slots, P(), P(), P(), P(), plane, plane, plane)
    return jax.shard_map(
        body, mesh=mesh, in_specs=in_specs, out_specs=(field, slots), check_vma=False
    )
```

```python
import jax
import jax.numpy as jnp
from jax import lax
from jax.experimental import pallas as pl
from jax.experimental.pallas import tpu as pltpu
from jax.sharding import PartitionSpec as P

GROUP_AXES = ("lat", "span")
MIB = 1024 * 1024
ROWS_MLP = 2048
PART = 512
VMEM_LIMIT = 60 * MIB
SUB = 8


def swapped(edge, axis, first, wrap):
    count = lax.axis_size(axis)
    pairs = [(i, (i + 1) % count) for i in range(first, count if wrap else count - 1, 2)]
    return lax.ppermute(edge, axis, pairs + [(j, i) for i, j in pairs])


def exchange(rows):
    return lax.all_to_all(rows, GROUP_AXES, split_axis=0, concat_axis=0, tiled=True)


def tile_row(y, half):
    return (y // SUB) * (2 * SUB) + half * SUB + y % SUB


def one_hot(index, size):
    lanes = index.shape[1]
    step = 2 * SUB
    index = jnp.broadcast_to(index, (step, lanes)).astype(jnp.int16)
    place = lax.broadcasted_iota(jnp.int32, (step, lanes), 0).astype(jnp.int16)
    one, zero = jnp.ones((step, lanes), jnp.bfloat16), jnp.zeros((step, lanes), jnp.bfloat16)
    blocks = [
        jnp.where(index == place + jnp.int16(start), one, zero) for start in range(0, size, step)
    ]
    return jnp.concatenate(blocks, axis=0)


def log2(size):
    return size.bit_length() - 1


def dispatch_kernel(
    ny,
    nx,
    dest,
    slot,
    convect,
    state_hbm,
    w_in_hbm,
    w_mid_hbm,
    w_deep_hbm,
    slots,
    lat_even,
    lat_odd,
    lon_even,
    lon_odd,
    target,
    filled,
    half_in,
    half_mid,
    half_deep,
    state,
    w_in,
    w_mid,
    w_deep,
    chosen,
    choice,
    total,
    edges,
    arrived,
):
    load = pltpu.make_async_copy(state_hbm, state, arrived.at[0])
    load.start()
    loads = [
        pltpu.make_async_copy(w_in_hbm, w_in, arrived.at[1]),
        pltpu.make_async_copy(w_mid_hbm, w_mid, arrived.at[2]),
        pltpu.make_async_copy(w_deep_hbm, w_deep, arrived.at[3]),
    ]
    for weights in loads:
        weights.start()
    width = state.shape[0] // (ny * 2)
    lanes = nx // 2
    lower = choice.shape[1]
    uppers = chosen.shape[2] // width
    depth = choice.shape[2]
    lines = depth // nx
    steps = ny // lines
    group = filled.shape[0]
    capacity = ny * nx // group
    shift, mask = log2(lower), lower - 1
    live = convect[...] > 0
    goal = jnp.where(live, dest[...] * capacity + slot[...], ny * nx)
    owner = goal >> log2(capacity)
    owners = lax.broadcasted_iota(jnp.int32, (group, nx), 0)
    counts = jnp.zeros((group, nx), jnp.int32)
    for y in range(ny):
        counts += (owners == owner[y : y + 1]).astype(jnp.int32)
    filled[...] = jnp.broadcast_to(jnp.sum(counts, axis=1, keepdims=True), filled.shape)
    for half in range(2):
        target[half] = goal[:, half * lanes : (half + 1) * lanes]
    goals = goal.T
    load.wait()

    def build(g, b):
        for line in range(lines):
            y = g * lines + line
            choice[b, :, pl.ds(line * nx, nx)] = one_hot(goal[y : y + 1] & mask, lower)
            upper = jnp.broadcast_to(goals[:, y : y + 1] >> shift, (nx, width)).astype(jnp.int16)
            for half in range(2):
                part = slice(half * lanes, (half + 1) * lanes)
                values = state[pl.ds(tile_row(y, half), width, stride=2 * ny), :].T
                if half == 0:
                    edges[pl.ds(y, 1), :] = values[:1]
                else:
                    edges[pl.ds(ny + y, 1), :] = values[lanes - 1 :]
                values = values.astype(jnp.bfloat16)
                rows = pl.ds(line * nx + half * lanes, lanes)
                for h in range(uppers):
                    chosen[b, rows, pl.ds(h * width, width)] = jnp.where(
                        upper[part] == h, values, jnp.zeros_like(values)
                    )

    def multiply(g, b):
        product = jnp.dot(choice[b], chosen[b], preferred_element_type=jnp.float32)
        if g == 0:
            total[...] = product
        else:
            total[...] += product

    build(0, 0)
    for g in range(steps):
        if g < steps - 1:
            build(g + 1, (g + 1) % 2)
        multiply(g, g % 2)
    for h in range(uppers):
        slots[pl.ds(h * lower, lower), :] = total[:, pl.ds(h * width, width)].astype(slots.dtype)

    odd = lax.axis_index("lat") % 2 == 1
    for half in range(2):
        part = pl.ds(half * lanes, lanes)
        south = state[pl.ds(tile_row(0, half), width, stride=2 * ny), :]
        north = state[pl.ds(tile_row(ny - 1, half), width, stride=2 * ny), :]
        lat_even[:, part] = jnp.where(odd, south, north).astype(lat_even.dtype)
        lat_odd[:, part] = jnp.where(odd, north, south).astype(lat_odd.dtype)
    odd = lax.axis_index("span") == 1
    west, east = edges[pl.ds(0, ny), :], edges[pl.ds(ny, ny), :]
    lon_even[...] = jnp.where(odd, west, east).astype(lon_even.dtype)
    lon_odd[...] = jnp.where(odd, east, west).astype(lon_odd.dtype)
    for weights in loads:
        weights.wait()
    for half, weights in ((half_in, w_in), (half_mid, w_mid), (half_deep, w_deep)):
        half[...] = weights[...] * jnp.bfloat16(0.5)


def dispatch(dest, slot, convect, state, weights, group):
    ny, nx = dest.shape
    width, count = state.shape[0] // (ny * 2), ny * nx
    uppers, depth = 4, 4 * nx
    lower = count // uppers
    vmem = pl.BlockSpec(memory_space=pltpu.VMEM)
    kernel = lambda *refs: dispatch_kernel(ny, nx, *refs)
    shape = jax.ShapeDtypeStruct
    return pl.pallas_call(
        kernel,
        out_shape=(
            shape((count, width), jnp.bfloat16),
            shape((width, nx), jnp.bfloat16),
            shape((width, nx), jnp.bfloat16),
            shape((ny, width), jnp.bfloat16),
            shape((ny, width), jnp.bfloat16),
            shape((2, ny, nx // 2), jnp.int32),
            shape((group, width), jnp.int32),
        )
        + tuple(shape(w.shape, w.dtype) for w in weights),
        in_specs=[vmem, vmem, vmem] + [pl.BlockSpec(memory_space=pl.ANY)] * 4,
        out_specs=(vmem,) * 10,
        scratch_shapes=[
            pltpu.VMEM(state.shape, jnp.float32),
        ]
        + [pltpu.VMEM(w.shape, w.dtype) for w in weights]
        + [
            pltpu.VMEM((2, depth, uppers * width), jnp.bfloat16),
            pltpu.VMEM((2, lower, depth), jnp.bfloat16),
            pltpu.VMEM((lower, uppers * width), jnp.float32),
            pltpu.VMEM((2 * ny, width), jnp.float32),
            pltpu.SemaphoreType.DMA((4,)),
        ],
        compiler_params=pltpu.CompilerParams(vmem_limit_bytes=63 * MIB),
        cost_estimate=pl.CostEstimate(
            flops=2 * count * count * width,
            bytes_accessed=6 * count * width,
            transcendentals=0,
        ),
        name="dispatch",
    )(dest, slot, convect, state, *weights)


def silu_of_half(half):
    return half + half * jnp.tanh(half)


def network_kernel(
    capacity,
    filled,
    columns,
    recalled,
    half_in,
    half_mid_hbm,
    half_deep_hbm,
    w_out_hbm,
    tend,
    renewed,
    half_mid,
    half_deep,
    w_out,
    arrived,
):
    loads = [
        pltpu.make_async_copy(half_mid_hbm, half_mid, arrived.at[0]),
        pltpu.make_async_copy(half_deep_hbm, half_deep, arrived.at[1]),
        pltpu.make_async_copy(w_out_hbm, w_out, arrived.at[2]),
    ]
    for load in loads:
        load.start()
    width = columns.shape[1]
    size, wide = PART, half_in.shape[1]
    parts = columns.shape[0] // size
    rows = [pl.ds(p * size, size) for p in range(parts)]
    values = [[columns[r, :], recalled[r, :]] for r in rows]
    waiting = []

    def settle():
        sums, kept = waiting.pop(0)
        kept.append(silu_of_half(sums).astype(jnp.bfloat16))

    for i, weights in enumerate((half_in, half_mid, half_deep)):
        if i > 0:
            loads[i - 1].wait()
        following = [[] for _ in rows]
        for p in range(parts):
            joined = jnp.concatenate(values[p], axis=1)
            for n in range(weights.shape[1] // wide):
                piece = weights[:, pl.ds(n * wide, wide)]
                sums = jnp.dot(joined, piece, preferred_element_type=jnp.float32)
                waiting.append((sums, following[p]))
                if len(waiting) > 1:
                    settle()
        values = following
    settle()
    loads[2].wait()
    owners = size // capacity
    place = lax.broadcasted_iota(jnp.int32, (capacity, width), 0)
    for p in range(parts):
        joined = jnp.concatenate(values[p], axis=1)
        result = jnp.dot(joined, w_out[...], preferred_element_type=jnp.float32)
        tend[rows[p], :] = result[:, :width].astype(tend.dtype)
        for o in range(owners):
            part = pl.ds(p * size + o * capacity, capacity)
            live = place < filled[pl.ds(p * owners + o, 1), :]
            update = result[o * capacity : (o + 1) * capacity, width:]
            old = recalled[part, :].astype(jnp.float32)
            renewed[part, :] = (old + jnp.where(live, update, 0.0)).astype(renewed.dtype)


def network(filled, columns, recalled, w_in, w_mid, w_deep, w_out):
    count, width = columns.shape
    capacity = count // filled.shape[0]
    rows = pl.BlockSpec((ROWS_MLP, width), lambda i: (i, 0))
    counts = pl.BlockSpec((ROWS_MLP // capacity, width), lambda i: (i, 0))
    whole = lambda w: pl.BlockSpec(w.shape, lambda i: (0, 0))
    kernel = lambda *refs: network_kernel(capacity, *refs)
    weights = (w_in, w_mid, w_deep, w_out)
    return pl.pallas_call(
        kernel,
        grid=(count // ROWS_MLP,),
        out_shape=(
            jax.ShapeDtypeStruct((count, width), jnp.bfloat16),
            jax.ShapeDtypeStruct((count, width), jnp.bfloat16),
        ),
        in_specs=[counts, rows, rows, whole(w_in)] + [pl.BlockSpec(memory_space=pl.ANY)] * 3,
        out_specs=(rows, rows),
        scratch_shapes=[pltpu.VMEM(w.shape, w.dtype) for w in weights[1:]]
        + [pltpu.SemaphoreType.DMA((3,))],
        compiler_params=pltpu.CompilerParams(vmem_limit_bytes=VMEM_LIMIT),
        cost_estimate=pl.CostEstimate(
            flops=2 * count * sum(w.size for w in weights),
            bytes_accessed=8 * count * width + 2 * sum(w.size for w in weights),
            transcendentals=count * 3 * w_mid.shape[0],
        ),
        name="network",
    )(filled, columns, recalled, *weights)


def finish_kernel(
    ny,
    nx,
    target,
    tend_hbm,
    state_hbm,
    winds_hbm,
    lat_even,
    lat_odd,
    lon_even,
    lon_odd,
    out_hbm,
    tend,
    state,
    winds,
    table,
    low,
    high,
    moved,
    flow,
    arrived,
    left_over,
):
    width = state.shape[0] // (ny * 2)
    lanes = nx // 2
    subs = ny // SUB
    levels = winds.shape[0] // (4 * ny)
    count = ny * nx
    pitch = moved.shape[0] // width
    copies = [
        pltpu.make_async_copy(tend_hbm, tend, arrived.at[0]),
        pltpu.make_async_copy(state_hbm, state, arrived.at[1]),
        pltpu.make_async_copy(winds_hbm, winds, arrived.at[2]),
    ]
    for copy in copies:
        copy.start()
    odd = lax.axis_index("span") == 1
    evens, odds = lon_even[...].astype(jnp.float32), lon_odd[...].astype(jnp.float32)
    west = jnp.where(odd, evens, odds)
    east = jnp.where(odd, odds, evens)
    odd = lax.axis_index("lat") % 2 == 1
    for half in range(2):
        part = pl.ds(half * lanes, lanes)
        evens, odds = lat_even[:, part].astype(jnp.float32), lat_odd[:, part].astype(jnp.float32)
        low[half] = jnp.where(odd, evens, odds)
        high[half] = jnp.where(odd, odds, evens)
    lower = table.shape[1]
    uppers = table.shape[0] // width
    shift, mask = log2(lower), lower - 1
    copies[0].wait()
    for h in range(uppers):
        rows = tend[pl.ds(h * lower, lower), :].astype(jnp.float32)
        table[pl.ds(h * width, width), :] = rows.T.astype(table.dtype)

    lane = lax.broadcasted_iota(jnp.int32, (SUB, lanes), 1)
    line = lax.broadcasted_iota(jnp.int32, (SUB, lanes), 0)
    tiles = [(sub, half) for sub in range(subs) for half in range(2)]

    def block(r, sub, half):
        return pl.ds(r * (2 * ny) + (sub * 2 + half) * SUB, SUB)

    def move(y):
        index = jnp.concatenate([target[half, pl.ds(y, 1), :] for half in range(2)], axis=1)
        wanted = jnp.where(index == count, -1, index & mask)
        candidates = jnp.dot(
            table[...], one_hot(wanted, lower), preferred_element_type=jnp.float32
        ).reshape(uppers, width // SUB, SUB, nx)
        upper = jnp.broadcast_to(index >> shift, (SUB, nx))
        change = candidates[0]
        for h in range(1, uppers):
            change = jnp.where((upper == h)[None], candidates[h], change)
        change = change.reshape(width, nx)
        for half in range(2):
            place = pl.ds(tile_row(y, half), width, stride=pitch)
            moved[place, :] = change[:, half * lanes : (half + 1) * lanes]

    def advect(k):
        zonal = {t: winds[block(k, *t), :] for t in tiles}
        meridional = {t: winds[block(levels + k, *t), :] for t in tiles}
        for f in range(width // levels):
            r = f * levels + k
            s = {t: state[block(r, *t), :] for t in tiles}
            first = pltpu.roll(west, (width - r) % width, axis=1)
            last = pltpu.roll(east, width - 1 - r, axis=1)
            up = {t: pltpu.roll(s[t], 1, axis=1) for t in tiles}
            down = {t: pltpu.roll(s[t], lanes - 1, axis=1) for t in tiles}
            rise = {t: pltpu.roll(s[t], 1, axis=0) for t in tiles}
            fall = {t: pltpu.roll(s[t], SUB - 1, axis=0) for t in tiles}
            for sub, half in tiles:
                t = (sub, half)
                edge = slice(sub * SUB, (sub + 1) * SUB)
                left = jnp.where(lane == 0, up[sub, 0] if half else first[edge], up[t])
                right = jnp.where(lane == lanes - 1, last[edge] if half else down[sub, 1], down[t])
                under = rise[sub - 1, half] if sub else low[half, pl.ds(r, 1), :]
                over = fall[sub + 1, half] if sub < subs - 1 else high[half, pl.ds(r, 1), :]
                below = jnp.where(line == 0, under, rise[t])
                above = jnp.where(line == SUB - 1, over, fall[t])
                flow[block(r, *t), :] = (
                    s[t]
                    - jnp.maximum(zonal[t], 0.0) * (s[t] - left)
                    - jnp.minimum(zonal[t], 0.0) * (right - s[t])
                    - jnp.maximum(meridional[t], 0.0) * (s[t] - below)
                    - jnp.minimum(meridional[t], 0.0) * (above - s[t])
                )

    ahead = 2
    share = levels // (ny - ahead) + 1
    for y in range(ny):
        move(y)
        if y == ahead - 1:
            copies[1].wait()
            copies[2].wait()
        start = (y - ahead) * share
        for k in range(max(start, 0), max(min(start + share, levels), 0)):
            advect(k)
    pieces = left_over.shape[0]
    size = state.shape[0] // pieces
    sends = []
    for p in range(pieces):
        rows = pl.ds(p * size, size)
        for r in range(p * width // pieces, (p + 1) * width // pieces):
            here = pl.ds(r * 2 * ny, 2 * ny)
            flow[here, :] = flow[here, :] + moved[pl.ds(r * pitch, 2 * ny), :]
        sends.append(pltpu.make_async_copy(flow.at[rows, :], out_hbm.at[rows, :], left_over.at[p]))
        sends[-1].start()
    for send in sends:
        send.wait()


def finish(target, tend, state, winds, *edges):
    _, ny, lanes = target.shape
    nx = 2 * lanes
    count, width = tend.shape
    uppers = 8
    vmem = pl.BlockSpec(memory_space=pltpu.VMEM)
    hbm = pl.BlockSpec(memory_space=pl.ANY)
    kernel = lambda *refs: finish_kernel(ny, nx, *refs)
    return pl.pallas_call(
        kernel,
        out_shape=jax.ShapeDtypeStruct(state.shape, jnp.float32),
        in_specs=[vmem, hbm, hbm, hbm, vmem, vmem, vmem, vmem],
        out_specs=hbm,
        scratch_shapes=[
            pltpu.VMEM(tend.shape, tend.dtype),
            pltpu.VMEM(state.shape, jnp.float32),
            pltpu.VMEM(winds.shape, jnp.float32),
            pltpu.VMEM((uppers * width, count // uppers), jnp.bfloat16),
            pltpu.VMEM((2, width, lanes), jnp.float32),
            pltpu.VMEM((2, width, lanes), jnp.float32),
            pltpu.VMEM((width * (2 * ny + SUB), lanes), jnp.float32),
            pltpu.VMEM(state.shape, jnp.float32),
            pltpu.SemaphoreType.DMA((3,)),
            pltpu.SemaphoreType.DMA((4,)),
        ],
        compiler_params=pltpu.CompilerParams(vmem_limit_bytes=56 * MIB),
        cost_estimate=pl.CostEstimate(
            flops=2 * count * count * width,
            bytes_accessed=14 * count * width,
            transcendentals=0,
        ),
        name="finish",
    )(target, tend, state, winds, *edges)


def to_tiles(field):
    fields, levels, ny, nx = field.shape
    tiles = field.reshape(fields * levels, ny // SUB, SUB, 2, nx // 2)
    return tiles.transpose(0, 1, 3, 2, 4).reshape(fields * levels * ny * 2, nx // 2)


def from_tiles(tiles, shape):
    fields, levels, ny, nx = shape
    field = tiles.reshape(fields * levels, ny // SUB, 2, SUB, nx // 2)
    return field.transpose(0, 1, 3, 2, 4).reshape(shape)


def body(state, winds, memory, w_in, w_mid, w_deep, w_out, dest, slot, convect):
    group = lax.axis_size(GROUP_AXES)

    recalled = exchange(memory)
    flat_state, flat_winds = to_tiles(state), to_tiles(winds)
    columns, lat_even, lat_odd, lon_even, lon_odd, target, filled, *halves = dispatch(
        dest, slot, convect, flat_state, (w_in, w_mid, w_deep), group
    )
    loop = ("lon", "span")
    lon_even = swapped(lon_even, loop, 0, True)
    lon_odd = swapped(lon_odd, loop, 1, True)
    lat_even = swapped(lat_even, "lat", 0, False)
    lat_odd = swapped(lat_odd, "lat", 1, False)
    tend, renewed = network(filled, columns, recalled, *halves, w_out)
    edges = (lat_even, lat_odd, lon_even)
    renewed, edges = lax.optimization_barrier((renewed, edges))
    new_memory = exchange(renewed)
    new_state = finish(target, tend, flat_state, flat_winds, *edges, lon_odd)
    return from_tiles(new_state, state.shape), new_memory


def solution(mesh):
    field = P(None, None, "lat", ("lon", "span"))
    slots = P(("lon", "lat", "span"), None)
    plane = P("lat", ("lon", "span"))
    in_specs = (field, field, slots, P(), P(), P(), P(), plane, plane, plane)
    return jax.shard_map(
        body, mesh=mesh, in_specs=in_specs, out_specs=(field, slots), check_vma=False
    )
```
